256 devices in a mesh: nodes: 256 (over x, z, y, core).
Axes of the slice: x: 4, y: 4, z: 8, core: 2. Of those that a mesh axis runs over, the one named last changes fastest.
Arguments:
- features: bfloat16 [131072, 512], P('nodes'), may hold values from -6 to 6
- norm_gain: float32 [512], replicated, may hold values from 0.25 to 1.75
- w_query: bfloat16 [512, 512], replicated, may hold values from -0.25 to 0.25
- key_weight: bfloat16 [512, 512], replicated, may hold values from -0.25 to 0.25
- value_weight: bfloat16 [512, 512], replicated, may hold values from -0.25 to 0.25
- w_out: bfloat16 [512, 512], replicated, may hold values from -0.25 to 0.25
- virtual_states: bfloat16 [256, 128], P('nodes'), may hold values from -6 to 6
- block_pairs: int32 [4096, 2], P('nodes'), may hold values from 0 to 3, as said below
- block_masks: int32 [4096, 128, 128], P('nodes'), may hold values 0 or 1
- pair_counts: int32 [256], P('nodes'), may hold values from 2 to 16
- partners: int32 [256, 4, 4], P('nodes'), may hold values from 0 to 3, as said below
Outputs:
- attended: bfloat16 [131072, 512], P('nodes')
The draws below stay inside these ranges and needn't reach their ends.
Inputs may be any that keep to these rules, and one draw needn't show every extreme that they name: `block_pairs`: within one device the 16 slots name distinct (query block, key block) pairs. `partners`: for each m and each device pair (d, d xor 2^bit_m) the two rows are inverse permutations of the 4 local blocks.
All inputs are finite; a program needn't handle non-finite values. No bound on the sum of `block_masks` on one device may be relied on, other than what follows from the above.
Results may differ from the reference program's by a relative error of at most 0.0084.
Values may be sent and summed in bfloat16 or wider, within the bound.
A program may use at most 64 MiB of HBM per device.

```python
import jax
import jax.numpy as jnp
from jax import lax

D = 512
HEAD_COUNT = 8
BLK = 128
DEVICE_BLOCKS = 4
PAIRS = 16
VIRTUAL_NODES = 64
NODES = 131072
N_NODES = 256
DEVICES = 256


def draw_block_pairs(key, part):
    key = jax.random.fold_in(key, 11)
    device_keys = jax.random.split(key, DEVICES)

    def per_device(device_key):
        shuffled = jax.random.permutation(device_key, DEVICE_BLOCKS * DEVICE_BLOCKS)[:PAIRS]
        return jnp.stack([shuffled // DEVICE_BLOCKS, shuffled % DEVICE_BLOCKS], axis=-1)
    return jax.vmap(per_device)(device_keys).reshape(DEVICES * PAIRS, 2).astype(jnp.int32)


def draw_pair_counts(key, part):
    key = jax.random.fold_in(key, 12)
    first_key, second_key, third_key = jax.random.split(key, 3)
    first_roll = jax.random.randint(first_key, (DEVICES,), 0, PAIRS - 1)
    second_roll = jax.random.randint(second_key, (DEVICES,), 0, PAIRS - 1)
    counts_drawn = 2 + first_roll * second_roll // (PAIRS - 2)
    busiest = jax.random.randint(third_key, (), 0, DEVICES)
    device_ids = jnp.arange(DEVICES, dtype=jnp.int32)
    return jnp.where(device_ids == busiest, PAIRS, counts_drawn).astype(jnp.int32)


def draw_partners(key, part):
    key = jax.random.fold_in(key, 13)
    logn = DEVICES.bit_length() - 1
    match_bits = (0, 1, logn - 2, logn - 1)
    device_ids = jnp.arange(DEVICES, dtype=jnp.int32)
    tables = []
    for matching in range(4):
        partner_id = jnp.bitwise_xor(device_ids, 1 << match_bits[matching])
        lower_id = jnp.minimum(device_ids, partner_id)

        def per_device(device_id, lower):
            pair_key = jax.random.fold_in(jax.random.fold_in(key, matching), lower)
            shuffled = jax.random.permutation(pair_key, DEVICE_BLOCKS)
            inverse = jnp.argsort(shuffled)
            return jnp.where(device_id == lower, shuffled, inverse)
        tables.append(jax.vmap(per_device)(device_ids, lower_id))
    return jnp.stack(tables, axis=1).astype(jnp.int32)


def touch_ends(array, stream_key, smallest, top_value):
    dims = array.shape
    spot = [jax.random.randint(jax.random.fold_in(stream_key, axis), (), 0, dims[axis]) for axis in range(len(dims))]
    array = array.at[tuple(spot)].set(smallest)
    longest = dims.index(max(dims))
    spot[longest] = (spot[longest] + 1) % dims[longest]
    return array.at[tuple(spot)].set(top_value)


def block_scale(own_key, extent, pieces, smallest, top_value):
    loudness, own = 1.0, jax.random.fold_in(own_key, 6)
    for position, parts in pieces:
        heights = jnp.exp(jax.random.uniform(jax.random.fold_in(own, position), (parts,), jnp.float32, smallest / len(pieces), top_value / len(pieces)))
        loudness = loudness * jnp.repeat(heights, extent[position] // parts).reshape([-1 if axis == position else 1 for axis in range(len(extent))])
    return loudness


def gaussian(rng, dims, scale, reach, pieces=(), kind=jnp.bfloat16):
    gain = block_scale(rng, dims, pieces, -0.22, 0.18) if pieces else 1.0
    result = jax.random.normal(rng, dims, jnp.float32) * scale * gain
    return jnp.minimum(jnp.maximum(result, -reach), reach).astype(kind)


def setup_inputs(seed: int = 0) -> dict:
    splits = jax.random.split(jax.random.key(seed), 12)
    return {
        "features": gaussian(splits[0], (NODES, D), 1.0, 6.0, ((0, 256),)),
        "norm_gain": jnp.clip(1.0 + 0.15 * jax.random.normal(splits[1], (D,), jnp.float32), 0.25, 1.75),
        "w_query": gaussian(splits[2], (D, D), D ** -0.5, 0.25),
        "key_weight": gaussian(splits[3], (D, D), D ** -0.5, 0.25),
        "value_weight": gaussian(splits[4], (D, D), D ** -0.5, 0.25),
        "w_out": gaussian(splits[5], (D, D), D ** -0.5, 0.25),
        "virtual_states": gaussian(splits[6], (VIRTUAL_NODES * 4, D // 4), 1.0, 6.0, ((0, 256),)),
        "block_pairs": draw_block_pairs(jax.random.fold_in(splits[11], 71), 0),
        "block_masks": touch_ends((jax.random.randint(splits[8], (DEVICES * PAIRS, BLK, BLK), 0, 8) < 1).astype(jnp.int32), jax.random.fold_in(splits[8], 1), 0, 1),
        "pair_counts": draw_pair_counts(jax.random.fold_in(splits[11], 71), 0),
        "partners": draw_partners(jax.random.fold_in(splits[11], 71), 0),
    }


EPSILON = 1e-05

def norm_rows(rows, norm_gain):
    floats = rows.astype(jnp.float32)
    center = floats - lax.optimization_barrier(jnp.mean(floats, axis=-1, keepdims=True))
    variance = lax.optimization_barrier(jnp.mean(center * center, axis=-1, keepdims=True))
    return (center * lax.rsqrt(variance + EPSILON) * norm_gain.astype(jnp.float32)).astype(jnp.bfloat16)

def rounded(weights):
    return lax.optimization_barrier(weights.astype(jnp.bfloat16)).astype(jnp.float32)

def attend(state, queries, keys_in, values_in, score_scale, keep):
    numerator, denominator = state
    scores = jnp.einsum('bhqd,bhkd->bhqk', queries.astype(jnp.float32), keys_in.astype(jnp.float32)) * score_scale
    weights = jnp.exp(scores) * keep
    denominator = denominator + lax.optimization_barrier(jnp.sum(weights, axis=-1))
    numerator = numerator + jnp.einsum('bhqk,bhkd->bhqd', rounded(weights), values_in.astype(jnp.float32))
    return (numerator, denominator)

def reference(features, norm_gain, w_query, key_weight, value_weight, w_out, virtual_states, block_pairs, block_masks, pair_counts, partners):
    device_count = N_NODES
    head_width = D // HEAD_COUNT
    score_scale = float(head_width) ** (-0.5)
    logn = device_count.bit_length() - 1
    match_bits = (0, 1, logn - 2, logn - 1)
    normed = norm_rows(features, norm_gain)

    def split_heads(rows):
        return rows.reshape(device_count, DEVICE_BLOCKS, BLK, HEAD_COUNT, head_width).transpose(0, 1, 3, 2, 4)
    q_heads = split_heads(jnp.dot(normed, w_query, preferred_element_type=jnp.float32).astype(jnp.bfloat16))
    k_heads = split_heads(jnp.dot(normed, key_weight, preferred_element_type=jnp.float32).astype(jnp.bfloat16))
    v_heads = split_heads(jnp.dot(normed, value_weight, preferred_element_type=jnp.float32).astype(jnp.bfloat16))
    virtual_norm = norm_rows(virtual_states.reshape(VIRTUAL_NODES, D), norm_gain)
    virtual_keys = jnp.dot(virtual_norm, key_weight, preferred_element_type=jnp.float32).astype(jnp.bfloat16)
    virtual_values = jnp.dot(virtual_norm, value_weight, preferred_element_type=jnp.float32).astype(jnp.bfloat16)
    virtual_keys = virtual_keys.reshape(VIRTUAL_NODES, HEAD_COUNT, head_width).transpose(1, 0, 2)
    virtual_values = virtual_values.reshape(VIRTUAL_NODES, HEAD_COUNT, head_width).transpose(1, 0, 2)

    def device_rows(device):
        queries = q_heads[device]
        own_keys = k_heads[device]
        own_vals = v_heads[device]
        numerator = jnp.zeros((DEVICE_BLOCKS, HEAD_COUNT, BLK, head_width), jnp.float32)
        denominator = jnp.zeros((DEVICE_BLOCKS, HEAD_COUNT, BLK), jnp.float32)
        pair_rows = lax.dynamic_slice_in_dim(block_pairs, device * PAIRS, PAIRS, 0)
        mask_rows = lax.dynamic_slice_in_dim(block_masks, device * PAIRS, PAIRS, 0)
        valid = (jnp.arange(PAIRS, dtype=jnp.int32) < pair_counts[device]).astype(jnp.float32)
        keep = mask_rows[:, None].astype(jnp.float32) * valid[:, None, None, None]
        slot_state = (jnp.zeros((PAIRS, HEAD_COUNT, BLK, head_width), jnp.float32), jnp.zeros((PAIRS, HEAD_COUNT, BLK), jnp.float32))
        slot_num, slot_den = attend(slot_state, queries[pair_rows[:, 0]], own_keys[pair_rows[:, 1]], own_vals[pair_rows[:, 1]], score_scale, keep)
        numerator = numerator.at[pair_rows[:, 0]].add(slot_num)
        denominator = denominator.at[pair_rows[:, 0]].add(slot_den)
        for matching in range(4):
            partner_dev = jnp.bitwise_xor(device, 1 << match_bits[matching])
            partner_idx = partners[device, matching]
            far_keys = k_heads[partner_dev][partner_idx]
            far_vals = v_heads[partner_dev][partner_idx]
            numerator, denominator = attend((numerator, denominator), queries, far_keys, far_vals, score_scale, 1.0)
        broadened_keys = jnp.broadcast_to(virtual_keys[None], (DEVICE_BLOCKS, HEAD_COUNT, VIRTUAL_NODES, head_width))
        broadened_values = jnp.broadcast_to(virtual_values[None], (DEVICE_BLOCKS, HEAD_COUNT, VIRTUAL_NODES, head_width))
        numerator, denominator = attend((numerator, denominator), queries, broadened_keys, broadened_values, score_scale, 1.0)
        mixed = numerator / denominator[..., None]
        return mixed.transpose(0, 2, 1, 3).reshape(DEVICE_BLOCKS * BLK, D).astype(jnp.bfloat16)
    mixed_all = lax.map(device_rows, jnp.arange(device_count, dtype=jnp.int32)).reshape(NODES, D)
    return jnp.dot(mixed_all, w_out, preferred_element_type=jnp.float32).astype(jnp.bfloat16)
```

```python
import functools

import jax
import jax.numpy as jnp
from jax import lax
from jax.experimental import pallas as pl
from jax.experimental.pallas import tpu as pltpu
from jax.sharding import PartitionSpec as P

HEADS = 8
WIDTH = 512
HEAD = 64
BLK = 128
BLOCKS = 4
ROWS = BLK * BLOCKS
SLOTS = 16
VIRTUAL = 64
PAIR = 4
EPSILON = 1e-05
SCORE_SCALE = 1.4426950408889634 / 8.0
RELAY = 64
RELAYS = ROWS // RELAY
PER_BLOCK = BLK // RELAY
MESH = pl.DeviceIdType.MESH
BF = jnp.bfloat16
F32 = jnp.float32


def norm_rows(floats, gain):
    center = floats - jnp.mean(floats, axis=-1, keepdims=True)
    variance = jnp.mean(center * center, axis=-1, keepdims=True)
    return (center * lax.rsqrt(variance + EPSILON) * gain).astype(BF)


def scores(q, k2):
    return lax.dot_general(q, k2, (((1,), (1,)), ((), ())), preferred_element_type=F32)


def dot(a, b):
    return jnp.dot(a, b, preferred_element_type=F32)


def lane_halves(rows):
    lane = lax.broadcasted_iota(jnp.int32, (rows, BLK), 1)
    even = jnp.where(lane < HEAD, 1.0, 0.0).astype(BF)
    odd = jnp.where(lane < HEAD, 0.0, 1.0).astype(BF)
    return even, odd


def kernel(
    features, gain_ref, w_query, key_weight, value_weight, w_out, virtual_row, pairs, masks, counts, partners,
    out_ref,
    raw, normed, wq, wkv, wo, mask_raw, keep, qs, own_k, own_v, land_core, core_k, core_v, land, far_k, far_v,
    virt_k, virt_v, gather, near, far_acc,
    local_sem, send_row, recv_row, send_core, recv_core, send_y, recv_y, send_x, recv_x, send_relay, recv_relay,
):
    me = lax.axis_index("nodes")
    core = me % 2
    y = (me // 2) % 4
    z = (me // 8) % 8
    x = me // 64
    y_near = y + 1 - 2 * (y % 2)
    x_near = x + 1 - 2 * (x % 2)

    def device(xx, zz, yy, cc):
        return xx * 64 + zz * 8 + yy * 2 + cc

    core_peer = device(x, z, y, 1 - core)
    y_peer = device(x, z, y_near, core)
    x_peer = device(x_near, z, y, core)
    relay_peer = device(3 - x, z, y, core)
    first = []
    for dx in range(4):
        for flip_y in range(2):
            for flip_core in range(2):
                if dx or flip_y or flip_core:
                    first.append(
                        device((x + dx) % 4, z, y_near if flip_y else y, 1 - core if flip_core else core)
                    )
    second = device(x, z, 3 - y, core)
    third = [device(x, (z + dz) % 8, y, core) for dz in range(1, 8)]
    peers = first + [second] + third

    barrier = pltpu.get_barrier_semaphore()
    for peer in peers:
        pl.semaphore_signal(barrier, inc=1, device_id=(peer,), device_id_type=MESH)

    def fetch(src, dst, index):
        copy = pltpu.make_async_copy(src, dst, local_sem.at[index])
        copy.start()
        return copy

    get_features = fetch(features, raw, 0)
    get_query = fetch(w_query, wq, 1)
    get_key = fetch(key_weight, wkv.at[:, pl.ds(0, WIDTH)], 2)
    get_value = fetch(value_weight, wkv.at[:, pl.ds(WIDTH, WIDTH)], 3)
    get_masks = fetch(masks, mask_raw, 4)
    get_out = fetch(w_out, wo, 5)

    gain = gain_ref[...]
    yc = y * 2 + core
    gather[x, z, pl.ds(yc, 1)] = virtual_row[...].astype(F32)
    get_features.wait()
    for block in range(BLOCKS):
        rows = pl.ds(block * BLK, BLK)
        normed[rows] = norm_rows(raw[rows].astype(F32), gain)

    def remote(src, dst, send, recv, peer):
        return pltpu.make_async_remote_copy(
            src_ref=src, dst_ref=dst, send_sem=send, recv_sem=recv, device_id=(peer,), device_id_type=MESH
        )

    def x_copy(r):
        c, part = r // PER_BLOCK, r % PER_BLOCK
        return remote(
            normed.at[pl.ds(r * RELAY, RELAY)],
            land.at[c, 1, pl.ds(part * RELAY, RELAY)],
            send_x.at[r], recv_x.at[r], x_peer,
        )

    def relay_copy(r):
        c, part = r // PER_BLOCK, r % PER_BLOCK
        return remote(
            land.at[c, 1, pl.ds(part * RELAY, RELAY)],
            land.at[c + 1, 2, pl.ds(part * RELAY, RELAY)],
            send_relay.at[r], recv_relay.at[r], relay_peer,
        )

    def y_copy(c):
        return remote(normed.at[pl.ds(c * BLK, BLK)], land.at[c, 0], send_y.at[c], recv_y.at[c], y_peer)

    copy_core = remote(normed, land_core, send_core.at[0], recv_core.at[0], core_peer)
    mine = gather.at[x, z, pl.ds(yc, 1)]
    copy_first = [remote(mine, mine, send_row.at[i], recv_row.at[i], peer) for i, peer in enumerate(first)]
    four = gather.at[:, z, pl.ds(4 * (y // 2), 4)]
    copy_second = remote(four, four, send_row.at[15], recv_row.at[15], second)
    plane = gather.at[:, z]
    copy_third = [remote(plane, plane, send_row.at[16 + i], recv_row.at[16 + i], peer) for i, peer in enumerate(third)]

    pl.semaphore_wait(barrier, len(peers))
    for copy in copy_first:
        copy.start()
    for c in range(BLOCKS):
        for part in range(PER_BLOCK):
            x_copy(c * PER_BLOCK + part).start()
        y_copy(c).start()
    copy_core.start()

    def relay(r):
        x_copy(r).wait_recv()
        relay_copy(r).start()

    even, odd = lane_halves(BLK)
    get_query.wait()
    for j in range(PAIR):
        part = dot(normed[...], wq[:, j * BLK:(j + 1) * BLK]) * SCORE_SCALE
        for b in range(BLOCKS):
            qs[b, j] = part[b * BLK:(b + 1) * BLK].astype(BF)

    def project(rows, place_k, place_v, blocks):
        for j in range(PAIR):
            part = dot(rows, wkv[:, j * BLK:(j + 1) * BLK])
            for b in range(blocks):
                piece = part[b * BLK:(b + 1) * BLK].astype(BF)
                ref = place_k(b, j)
                ref[0:BLK] = piece * even
                ref[BLK:2 * BLK] = piece * odd
            part = dot(rows, wkv[:, WIDTH + j * BLK:WIDTH + (j + 1) * BLK])
            for b in range(blocks):
                piece = part[b * BLK:(b + 1) * BLK].astype(BF)
                ref = place_v(b, j)
                ref[0:BLK] = piece * even
                ref[BLK:2 * BLK] = piece * odd

    get_key.wait()
    get_value.wait()
    project(normed[...], lambda b, j: own_k.at[j, b], lambda b, j: own_v.at[j, b], BLOCKS)

    ones = jnp.concatenate([even, odd], axis=0)

    def widen(v2):
        return jnp.concatenate([v2, ones], axis=1)

    get_masks.wait()
    live = counts[0]
    for qb in range(BLOCKS):
        for kb in range(BLOCKS):
            slot = jnp.int32(0)
            for s in range(SLOTS):
                slot = jnp.where((pairs[s, 0] == qb) & (pairs[s, 1] == kb), s, slot)
            alive = jnp.where(slot < live, 1, 0)
            keep[qb, kb] = (mask_raw[slot] * alive).astype(F32).astype(BF)

    for copy in copy_first:
        copy.wait_recv()
    copy_second.start()

    @pl.loop(0, PAIR)
    def _(j):
        for b in range(BLOCKS):
            q = qs[b, j]
            total = None
            for kb in range(BLOCKS):
                p = jnp.exp2(scores(q, own_k[j, kb])).astype(BF)
                mask = keep[b, kb]
                p = p * jnp.concatenate([mask, mask], axis=1)
                part = dot(p, widen(own_v[j, kb]))
                total = part if total is None else total + part
            near[b, j] = total

    copy_second.wait_recv()
    for copy in copy_third:
        copy.start()
    relay(0)

    copy_core.wait_recv()
    project(land_core[...], lambda b, j: core_k.at[b, j], lambda b, j: core_v.at[b, j], BLOCKS)
    relay(1)

    @pl.loop(0, PAIR)
    def _(j):
        for b in range(BLOCKS):
            key_block = partners[0, b]
            p = jnp.exp2(scores(qs[b, j], core_k[key_block, j])).astype(BF)
            near[b, j] += dot(p, widen(core_v[key_block, j]))

    def far_step(c, sources):
        lo, hi = sources[0], sources[-1] + 1
        rows = land[c, lo:hi].reshape((hi - lo) * BLK, WIDTH)
        project(rows, lambda b, j: far_k.at[lo + b, j], lambda b, j: far_v.at[lo + b, j], hi - lo)
        for m in sources:
            block = c - 1 if m == 2 else c
            target = jnp.int32(0)
            for b in range(BLOCKS):
                target = jnp.where(partners[m + 1, b] == block, b, target)
            for j in range(PAIR):
                p = jnp.exp2(scores(qs[target, j], far_k[m, j])).astype(BF)
                far_acc[m, block, j] = dot(p, widen(far_v[m, j]))

    def arrive(c):
        for part in range(PER_BLOCK):
            r = c * PER_BLOCK + part
            if not isinstance(c, int) or r > 1:
                relay(r)
        y_copy(c).wait_recv()

    def arrive_relayed(c):
        for part in range(PER_BLOCK):
            relay_copy(c * PER_BLOCK + part).wait_recv()

    arrive(0)
    far_step(0, (0, 1))

    @pl.loop(1, BLOCKS)
    def _(c):
        arrive(c)
        arrive_relayed(c - 1)
        far_step(c, (0, 1, 2))

    for copy in copy_third:
        copy.wait_recv()
    even_v, odd_v = lane_halves(VIRTUAL)
    ones_v = jnp.concatenate([even_v, odd_v], axis=0)
    table = gather.reshape(256, BLK)
    state = jnp.concatenate([table[pl.ds(i, VIRTUAL, stride=4), :] for i in range(4)], axis=1)
    virtual_norm = norm_rows(state, gain)
    virtual_kv = dot(virtual_norm, wkv[...]).astype(BF)
    for j in range(PAIR):
        piece = virtual_kv[:, j * BLK:(j + 1) * BLK]
        virt_k[j, 0:VIRTUAL] = piece * even_v
        virt_k[j, VIRTUAL:2 * VIRTUAL] = piece * odd_v
        piece = virtual_kv[:, WIDTH + j * BLK:WIDTH + (j + 1) * BLK]
        virt_v[j, 0:VIRTUAL] = piece * even_v
        virt_v[j, VIRTUAL:2 * VIRTUAL] = piece * odd_v

    @pl.loop(0, PAIR)
    def _(j):
        wide = jnp.concatenate([virt_v[j], ones_v], axis=1)
        for b in range(BLOCKS):
            p = jnp.exp2(scores(qs[b, j], virt_k[j])).astype(BF)
            near[b, j] += (
                dot(p, wide) + far_acc[0, partners[1, b], j] + far_acc[1, partners[2, b], j]
            )

    get_out.wait()
    arrive_relayed(BLOCKS - 1)
    far_step(BLOCKS, (2,))

    for b in range(BLOCKS):
        mixed = []
        for j in range(PAIR):
            total = near[b, j] + far_acc[2, partners[3, b], j]
            mixed.append((total[:, 0:BLK] / total[:, BLK:2 * BLK]).astype(BF))
        out_ref[b * BLK:(b + 1) * BLK] = dot(jnp.concatenate(mixed, axis=1), wo[...]).astype(BF)

    for copy in copy_first + [copy_second] + copy_third + [copy_core]:
        copy.wait_send()
    for r in range(RELAYS):
        x_copy(r).wait_send()
        relay_copy(r).wait_send()
    for c in range(BLOCKS):
        y_copy(c).wait_send()


def local(
    features, norm_gain, w_query, key_weight, value_weight, w_out, virtual_states, block_pairs, block_masks,
    pair_counts, partners,
):
    anywhere = pl.BlockSpec(memory_space=pl.ANY)
    vmem = pl.BlockSpec(memory_space=pltpu.VMEM)
    smem = pl.BlockSpec(memory_space=pltpu.SMEM)
    dma = pltpu.SemaphoreType.DMA
    return pl.pallas_call(
        kernel,
        out_shape=jax.ShapeDtypeStruct((ROWS, WIDTH), BF),
        in_specs=[anywhere, vmem, anywhere, anywhere, anywhere, anywhere, vmem, smem, anywhere, smem, smem],
        out_specs=vmem,
        scratch_shapes=[
            pltpu.VMEM((ROWS, WIDTH), BF),
            pltpu.VMEM((ROWS, WIDTH), BF),
            pltpu.VMEM((WIDTH, WIDTH), BF),
            pltpu.VMEM((WIDTH, 2 * WIDTH), BF),
            pltpu.VMEM((WIDTH, WIDTH), BF),
            pltpu.VMEM((SLOTS, BLK, BLK), jnp.int32),
            pltpu.VMEM((BLOCKS, BLOCKS, BLK, BLK), BF),
            pltpu.VMEM((BLOCKS, PAIR, BLK, BLK), BF),
            pltpu.VMEM((PAIR, BLOCKS, 2 * BLK, BLK), BF),
            pltpu.VMEM((PAIR, BLOCKS, 2 * BLK, BLK), BF),
            pltpu.VMEM((ROWS, WIDTH), BF),
            pltpu.VMEM((BLOCKS, PAIR, 2 * BLK, BLK), BF),
            pltpu.VMEM((BLOCKS, PAIR, 2 * BLK, BLK), BF),
            pltpu.VMEM((BLOCKS + 1, 3, BLK, WIDTH), BF),
            pltpu.VMEM((3, PAIR, 2 * BLK, BLK), BF),
            pltpu.VMEM((3, PAIR, 2 * BLK, BLK), BF),
            pltpu.VMEM((PAIR, BLK, BLK), BF),
            pltpu.VMEM((PAIR, BLK, BLK), BF),
            pltpu.VMEM((4, 8, 8, BLK), F32),
            pltpu.VMEM((BLOCKS, PAIR, BLK, 2 * BLK), F32),
            pltpu.VMEM((3, BLOCKS, PAIR, BLK, 2 * BLK), F32),
            dma((6,)),
            dma((23,)), dma((23,)),
            dma((1,)), dma((1,)),
            dma((BLOCKS,)), dma((BLOCKS,)),
            dma((RELAYS,)), dma((RELAYS,)),
            dma((RELAYS,)), dma((RELAYS,)),
        ],
        compiler_params=pltpu.CompilerParams(
            collective_id=0, has_side_effects=True, vmem_limit_bytes=48 * 1024 * 1024
        ),
        cost_estimate=pl.CostEstimate(flops=8_000_000_000, bytes_accessed=4_500_000, transcendentals=4_500_000),
        name="expander_layer",
    )(
        features, norm_gain.reshape(1, WIDTH), w_query, key_weight, value_weight, w_out, virtual_states,
        block_pairs, block_masks, pair_counts, partners.reshape(4, BLOCKS),
    )


def solution(mesh):
    placed = (
        P("nodes", None), P(), P(), P(), P(), P(), P("nodes", None), P("nodes", None), P("nodes", None, None),
        P("nodes"), P("nodes", None, None),
    )
    return jax.shard_map(local, mesh=mesh, in_specs=placed, out_specs=P("nodes", None), check_vma=False)
```

```python
import jax
import jax.numpy as jnp
from jax import lax
from jax.experimental import pallas as pl
from jax.experimental.pallas import tpu as pltpu
from jax.sharding import PartitionSpec as P

WIDTH = 512
HEAD = 64
BLK = 128
BLOCKS = 4
ROWS = BLK * BLOCKS
SLOTS = 16
VIRTUAL = 64
PAIR = 4
EPSILON = 1e-05
SCORE_SCALE = 1.4426950408889634 / 8.0
RELAY = 64
RELAYS = ROWS // RELAY
PER_BLOCK = BLK // RELAY
MESH = pl.DeviceIdType.MESH
BF = jnp.bfloat16
F32 = jnp.float32


def norm_rows(floats, gain):
    center = floats - jnp.mean(floats, axis=-1, keepdims=True)
    variance = jnp.mean(center * center, axis=-1, keepdims=True)
    return (center * lax.rsqrt(variance + EPSILON) * gain).astype(BF)


def scores(q, k2):
    return lax.dot_general(q, k2, (((1,), (1,)), ((), ())), preferred_element_type=F32)


def dot(a, b):
    return jnp.dot(a, b, preferred_element_type=F32)


def lane_halves(rows):
    lane = lax.broadcasted_iota(jnp.int32, (rows, BLK), 1)
    even = jnp.where(lane < HEAD, 1.0, 0.0).astype(BF)
    odd = jnp.where(lane < HEAD, 0.0, 1.0).astype(BF)
    return even, odd


def kernel(
    features, norm_gain, w_query, key_weight, value_weight, virtual_states, block_pairs, masks, counts, partner_blocks,
    out_ref,
    gain_ref, virtual_row, pairs, partners, raw, normed, wq, wkv, mask_raw, keep, qs, own_k, own_v, land_core, core_k,
    core_v, land, far_k, far_v, virt_k, virt_v, gather, near, far_acc, weights, far_w,
    local_sem, send_row, recv_row, send_core, recv_core, send_y, recv_y, send_x, recv_x, send_relay, recv_relay,
):
    me = lax.axis_index("nodes")
    core = me % 2
    y = (me // 2) % 4
    z = (me // 8) % 8
    x = me // 64
    y_near = y + 1 - 2 * (y % 2)
    x_near = x + 1 - 2 * (x % 2)

    def device(xx, zz, yy, cc):
        return xx * 64 + zz * 8 + yy * 2 + cc

    core_peer = device(x, z, y, 1 - core)
    y_peer = device(x, z, y_near, core)
    x_peer = device(x_near, z, y, core)
    relay_peer = device(3 - x, z, y, core)
    plane = []
    for dx in range(4):
        for flip_y in range(2):
            for flip_core in range(2):
                if dx or flip_y or flip_core:
                    plane.append(
                        device((x + dx) % 4, z, y_near if flip_y else y, 1 - core if flip_core else core)
                    )
    half = y // 2
    rank = jnp.where(z < 4, z * 2 + half, 8 + half * 4 + z - 4)

    def ranked(r):
        zz = jnp.where(r < 8, r // 2, 4 + r % 4)
        hh = jnp.where(r < 8, r % 2, (r - 8) // 4)
        return device(x, zz, jnp.where(hh == half, y, 3 - y), core)

    steps = range(1, 16)
    columns = {k: ranked((rank + k) % 16) for k in steps}

    def higher(k):
        return rank + k < 16

    barrier = pltpu.get_barrier_semaphore()
    for peer in plane:
        pl.semaphore_signal(barrier, inc=1, device_id=(peer,), device_id_type=MESH)
    for k in steps:
        @pl.when(higher(k))
        def _(k=k):
            pl.semaphore_signal(barrier, inc=1, device_id=(columns[k],), device_id_type=MESH)

    def fetch(src, dst, index):
        copy = pltpu.make_async_copy(src, dst, local_sem.at[index])
        copy.start()
        return copy

    get_features = fetch(features, raw, 0)
    get_gain = fetch(norm_gain, gain_ref, 1)
    get_row = fetch(virtual_states, virtual_row, 2)
    get_query = fetch(w_query, wq, 3)
    get_key = fetch(key_weight, wkv.at[:, pl.ds(0, WIDTH)], 4)
    get_value = fetch(value_weight, wkv.at[:, pl.ds(WIDTH, WIDTH)], 5)
    get_pairs = fetch(block_pairs, pairs, 6)
    get_partners = fetch(partner_blocks, partners, 7)
    get_masks = fetch(masks, mask_raw, 8)

    group = z * 2 + y // 2
    member = x * 4 + (y % 2) * 2 + core
    get_row.wait()
    gather[group, pl.ds(member, 1)] = virtual_row[...].astype(F32)
    get_gain.wait()
    gain = gain_ref[...]
    get_features.wait()
    for block in range(BLOCKS):
        rows = pl.ds(block * BLK, BLK)
        normed[rows] = norm_rows(raw[rows].astype(F32), gain)

    def remote(src, dst, send, recv, peer):
        return pltpu.make_async_remote_copy(
            src_ref=src, dst_ref=dst, send_sem=send, recv_sem=recv, device_id=(peer,), device_id_type=MESH
        )

    def x_copy(r):
        c, part = r // PER_BLOCK, r % PER_BLOCK
        return remote(
            normed.at[pl.ds(r * RELAY, RELAY)],
            land.at[c, 1, pl.ds(part * RELAY, RELAY)],
            send_x.at[r], recv_x.at[r], x_peer,
        )

    def relay_copy(r):
        c, part = r // PER_BLOCK, r % PER_BLOCK
        return remote(
            land.at[c, 1, pl.ds(part * RELAY, RELAY)],
            land.at[c + 1, 2, pl.ds(part * RELAY, RELAY)],
            send_relay.at[r], recv_relay.at[r], relay_peer,
        )

    def y_copy(c):
        return remote(normed.at[pl.ds(c * BLK, BLK)], land.at[c, 0], send_y.at[c], recv_y.at[c], y_peer)

    copy_core = remote(normed, land_core, send_core.at[0], recv_core.at[0], core_peer)
    mine = gather.at[group, pl.ds(member, 1)]
    copy_plane = [remote(mine, mine, send_row.at[i], recv_row.at[i], peer) for i, peer in enumerate(plane)]
    sixteen = gather.at[group]

    def column_copy(k):
        return remote(sixteen, sixteen, send_row.at[14 + k], recv_row.at[14 + k], columns[k])

    def column_arrived(k):
        column_copy(16 - k).wait_recv()

    def send_lower():
        for k in steps:
            @pl.when(jnp.logical_not(higher(k)))
            def _(k=k):
                column_copy(k).start()

    def answer_higher(late):
        for k in steps:
            crosses = (rank < 8) & (rank + k >= 8)
            @pl.when(higher(k) & (crosses if late else jnp.logical_not(crosses)))
            def _(k=k):
                column_arrived(k)
                column_copy(k).start()

    def hear_lower():
        for k in steps:
            @pl.when(jnp.logical_not(higher(k)))
            def _(k=k):
                column_arrived(k)

    def send_bulk():
        for copy in copy_plane:
            copy.start()
        for c in range(BLOCKS):
            for part in range(PER_BLOCK):
                x_copy(c * PER_BLOCK + part).start()
            y_copy(c).start()
        copy_core.start()

    def relay(r):
        x_copy(r).wait_recv()
        relay_copy(r).start()

    even, odd = lane_halves(BLK)
    ones = jnp.concatenate([even, odd], axis=0)

    def widen(v2):
        return jnp.concatenate([v2, ones], axis=1)

    def project(rows, place_k, place_v, blocks):
        for offset, place in ((0, place_k), (WIDTH, place_v)):
            for jj in range(0, PAIR, 2):
                part = dot(rows, wkv[:, offset + jj * BLK:offset + (jj + 2) * BLK])
                for j in range(jj, jj + 2):
                    for b in range(blocks):
                        piece = part[b * BLK:(b + 1) * BLK, (j - jj) * BLK:(j - jj + 1) * BLK].astype(BF)
                        ref = place(b, j)
                        ref[0:BLK] = piece * even
                        ref[BLK:2 * BLK] = piece * odd

    def own_queries():
        get_query.wait()
        for jj in range(0, PAIR, 2):
            part = dot(normed[...], wq[:, jj * BLK:(jj + 2) * BLK]) * SCORE_SCALE
            for j in range(jj, jj + 2):
                for b in range(BLOCKS):
                    qs[j, b] = part[b * BLK:(b + 1) * BLK, (j - jj) * BLK:(j - jj + 1) * BLK].astype(BF)

    def own_keys_values():
        get_key.wait()
        get_value.wait()
        project(normed[...], lambda b, j: own_k.at[j, b], lambda b, j: own_v.at[j, b], BLOCKS)

    def spread_masks():
        get_masks.wait()
        get_pairs.wait()
        get_partners.wait()
        live = counts[0]
        for qb in range(BLOCKS):
            for kb in range(BLOCKS):
                slot = jnp.int32(0)
                for s in range(SLOTS):
                    slot = jnp.where((pairs[0, s] == qb) & (pairs[1, s] == kb), s, slot)
                alive = jnp.where(slot < live, 1, 0)
                keep[qb, kb] = (mask_raw[slot] * alive).astype(F32).astype(BF)

    def attend_local(pair_range):
        for j in pair_range:
            q = qs[j].reshape(ROWS, BLK)
            for kb in range(BLOCKS):
                s = scores(q, own_k[j, kb])
                for b in range(BLOCKS):
                    mask = keep[b, kb]
                    p = jnp.exp2(s[b * BLK:(b + 1) * BLK]).astype(BF)
                    weights[j, b * BLK:(b + 1) * BLK, kb * 2 * BLK:(kb + 1) * 2 * BLK] = p * jnp.concatenate(
                        [mask, mask], axis=1
                    )
        for j in pair_range:
            v = jnp.concatenate([widen(own_v[j, kb]) for kb in range(BLOCKS)], axis=0)
            near[j] = dot(weights[j], v).reshape(BLOCKS, BLK, 2 * BLK)

    def project_core():
        project(land_core[...], lambda b, j: core_k.at[b, j], lambda b, j: core_v.at[b, j], BLOCKS)

    def attend_core():
        block = [partners[0, b] for b in range(BLOCKS)]
        for j in range(PAIR):
            for b in range(BLOCKS):
                weights[j, b * BLK:(b + 1) * BLK, 0:2 * BLK] = jnp.exp2(
                    scores(qs[j, b], core_k[block[b], j])
                ).astype(BF)
        for j in range(PAIR):
            for b in range(BLOCKS):
                near[j, b] += dot(weights[j, b * BLK:(b + 1) * BLK, 0:2 * BLK], widen(core_v[block[b], j]))

    def far_step(c, sources):
        lo, hi = sources[0], sources[-1] + 1
        rows = land[c, lo:hi].reshape((hi - lo) * BLK, WIDTH)
        project(rows, lambda b, j: far_k.at[lo + b, j], lambda b, j: far_v.at[lo + b, j], hi - lo)
        for m in sources:
            block = c - 1 if m == 2 else c
            target = jnp.int32(0)
            for b in range(BLOCKS):
                target = jnp.where(partners[m + 1, b] == block, b, target)
            for j in range(PAIR):
                far_w[m, j] = jnp.exp2(scores(qs[j, target], far_k[m, j])).astype(BF)
        for m in sources:
            block = c - 1 if m == 2 else c
            for j in range(PAIR):
                far_acc[m, block, j] = dot(far_w[m, j], widen(far_v[m, j]))

    def arrive_relayed(c):
        for part in range(PER_BLOCK):
            relay_copy(c * PER_BLOCK + part).wait_recv()

    def virtual_nodes():
        even_v, odd_v = lane_halves(VIRTUAL)
        ones_v = jnp.concatenate([even_v, odd_v], axis=0)
        table = gather.reshape(256, BLK)
        state = jnp.concatenate([table[pl.ds(i, VIRTUAL, stride=4), :] for i in range(4)], axis=1)
        virtual_kv = dot(norm_rows(state, gain), wkv[...]).astype(BF)
        for j in range(PAIR):
            for offset, ref in ((0, virt_k), (WIDTH, virt_v)):
                piece = virtual_kv[:, offset + j * BLK:offset + (j + 1) * BLK]
                ref[j, 0:VIRTUAL] = piece * even_v
                ref[j, VIRTUAL:2 * VIRTUAL] = piece * odd_v
        for j in range(PAIR):
            s = scores(qs[j].reshape(ROWS, BLK), virt_k[j])
            weights[j, :, 0:BLK] = jnp.exp2(s).astype(BF)
        for j in range(PAIR):
            wide = jnp.concatenate([virt_v[j], ones_v], axis=1)
            near[j] += dot(weights[j, :, 0:BLK], wide).reshape(BLOCKS, BLK, 2 * BLK)

    def add_far():
        for j in range(PAIR):
            for b in range(BLOCKS):
                near[j, b] += far_acc[0, partners[1, b], j] + far_acc[1, partners[2, b], j]

    def finish():
        for b in range(BLOCKS):
            for j in range(PAIR):
                total = near[j, b] + far_acc[2, partners[3, b], j]
                out_ref[b * BLK:(b + 1) * BLK, j * BLK:(j + 1) * BLK] = (
                    total[:, 0:BLK] / total[:, BLK:2 * BLK]
                ).astype(BF)

    pl.semaphore_wait(barrier, 15 + rank)
    send_bulk()
    own_queries()
    own_keys_values()
    spread_masks()
    attend_local((0, 1))
    for copy in copy_plane:
        copy.wait_recv()
    send_lower()
    relay(0)
    attend_local((2, 3))
    relay(1)
    copy_core.wait_recv()
    project_core()
    relay(2)
    attend_core()
    y_copy(0).wait_recv()
    far_step(0, (0, 1))
    relay(3)
    answer_higher(False)

    @pl.loop(1, BLOCKS)
    def _(c):
        y_copy(c).wait_recv()
        arrive_relayed(c - 1)
        far_step(c, (0, 1, 2))

        @pl.when(c < BLOCKS - 1)
        def _():
            for part in range(PER_BLOCK):
                relay((c + 1) * PER_BLOCK + part)

    for copy in copy_plane + [copy_core]:
        copy.wait_send()
    for r in range(RELAYS):
        x_copy(r).wait_send()
    for c in range(BLOCKS):
        y_copy(c).wait_send()
    answer_higher(True)
    hear_lower()
    virtual_nodes()
    add_far()
    for r in range(RELAYS - PER_BLOCK):
        relay_copy(r).wait_send()
    for k in steps:
        column_copy(k).wait_send()
    arrive_relayed(BLOCKS - 1)
    far_step(BLOCKS, (2,))
    finish()
    for r in range(RELAYS - PER_BLOCK, RELAYS):
        relay_copy(r).wait_send()


def local(
    features, norm_gain, w_query, key_weight, value_weight, w_out, virtual_states, block_pairs, block_masks,
    pair_counts, partners,
):
    dma = pltpu.SemaphoreType.DMA
    hbm = pl.BlockSpec(memory_space=pltpu.HBM)
    mixed = pl.pallas_call(
        kernel,
        out_shape=jax.ShapeDtypeStruct((ROWS, WIDTH), BF),
        in_specs=[hbm] * 8 + [pl.BlockSpec(memory_space=pltpu.SMEM), hbm],
        out_specs=pl.BlockSpec(memory_space=pltpu.VMEM),
        scratch_shapes=[
            pltpu.VMEM((1, WIDTH), F32),
            pltpu.VMEM((1, BLK), BF),
            pltpu.SMEM((2, SLOTS), jnp.int32),
            pltpu.SMEM((4, BLOCKS), jnp.int32),
            pltpu.VMEM((ROWS, WIDTH), BF),
            pltpu.VMEM((ROWS, WIDTH), BF),
            pltpu.VMEM((WIDTH, WIDTH), BF),
            pltpu.VMEM((WIDTH, 2 * WIDTH), BF),
            pltpu.VMEM((SLOTS, BLK, BLK), jnp.int32),
            pltpu.VMEM((BLOCKS, BLOCKS, BLK, BLK), BF),
            pltpu.VMEM((PAIR, BLOCKS, BLK, BLK), BF),
            pltpu.VMEM((PAIR, BLOCKS, 2 * BLK, BLK), BF),
            pltpu.VMEM((PAIR, BLOCKS, 2 * BLK, BLK), BF),
            pltpu.VMEM((ROWS, WIDTH), BF),
            pltpu.VMEM((BLOCKS, PAIR, 2 * BLK, BLK), BF),
            pltpu.VMEM((BLOCKS, PAIR, 2 * BLK, BLK), BF),
            pltpu.VMEM((BLOCKS + 1, 3, BLK, WIDTH), BF),
            pltpu.VMEM((3, PAIR, 2 * BLK, BLK), BF),
            pltpu.VMEM((3, PAIR, 2 * BLK, BLK), BF),
            pltpu.VMEM((PAIR, BLK, BLK), BF),
            pltpu.VMEM((PAIR, BLK, BLK), BF),
            pltpu.VMEM((16, 16, BLK), F32),
            pltpu.VMEM((PAIR, BLOCKS, BLK, 2 * BLK), F32),
            pltpu.VMEM((3, BLOCKS, PAIR, BLK, 2 * BLK), F32),
            pltpu.VMEM((PAIR, ROWS, 8 * BLK), BF),
            pltpu.VMEM((3, PAIR, BLK, 2 * BLK), BF),
            dma((9,)),
            dma((30,)), dma((30,)),
            dma((1,)), dma((1,)),
            dma((BLOCKS,)), dma((BLOCKS,)),
            dma((RELAYS,)), dma((RELAYS,)),
            dma((RELAYS,)), dma((RELAYS,)),
        ],
        compiler_params=pltpu.CompilerParams(
            collective_id=0, has_side_effects=True, vmem_limit_bytes=54500 * 1024
        ),
        cost_estimate=pl.CostEstimate(flops=8_000_000_000, bytes_accessed=4_500_000, transcendentals=4_500_000),
        name="expander_layer",
    )(
        features, norm_gain.reshape(1, WIDTH), w_query, key_weight, value_weight, virtual_states,
        block_pairs.T, block_masks, pair_counts, partners.reshape(4, BLOCKS),
    )
    return jnp.dot(mixed, w_out, preferred_element_type=F32).astype(BF)


def solution(mesh):
    placed = (
        P("nodes", None), P(), P(), P(), P(), P(), P("nodes", None), P("nodes", None), P("nodes", None, None),
        P("nodes"), P("nodes", None, None),
    )
    return jax.shard_map(local, mesh=mesh, in_specs=placed, out_specs=P("nodes", None), check_vma=False)
```

```python
import jax
import jax.numpy as jnp
from jax import lax
from jax.experimental import pallas as pl
from jax.experimental.pallas import tpu as pltpu
from jax.sharding import PartitionSpec as P

WIDTH = 512
HEAD = 64
BLK = 128
BLOCKS = 4
ROWS = BLK * BLOCKS
SLOTS = 16
VIRTUAL = 64
PAIR = 4
EPSILON = 1e-05
SCORE_SCALE = 1.4426950408889634 / 8.0
RELAY = 32
RELAYS = ROWS // RELAY
PER_BLOCK = BLK // RELAY
MESH = pl.DeviceIdType.MESH
BF = jnp.bfloat16
F32 = jnp.float32


def norm_rows(floats, gain):
    center = floats - jnp.mean(floats, axis=-1, keepdims=True)
    variance = jnp.mean(center * center, axis=-1, keepdims=True)
    return (center * lax.rsqrt(variance + EPSILON) * gain).astype(BF)


def scores(q, k2):
    return lax.dot_general(q, k2, (((1,), (1,)), ((), ())), preferred_element_type=F32)


def dot(a, b):
    return jnp.dot(a, b, preferred_element_type=F32)


def lane_halves(rows):
    lane = lax.broadcasted_iota(jnp.int32, (rows, BLK), 1)
    even = jnp.where(lane < HEAD, 1.0, 0.0).astype(BF)
    odd = jnp.where(lane < HEAD, 0.0, 1.0).astype(BF)
    return even, odd


def kernel(
    features, norm_gain, w_query, key_weight, value_weight, virtual_states, block_pairs, masks, counts, partner_blocks,
    out_ref,
    gain_ref, virtual_row, pairs, partners, raw, normed, wq, wkv, mask_raw, keep, qs, own_k, own_v, land_core, core_k,
    core_v, land, far_k, far_v, virt_k, virt_v, gather, near, far_acc, weights, far_w,
    local_sem, send_row, recv_row, send_core, recv_core, send_y, recv_y, send_x, recv_x, send_relay, recv_relay, entered, token,
):
    me = lax.axis_index("nodes")
    core = me % 2
    y = (me // 2) % 4
    z = (me // 8) % 8
    x = me // 64
    y_near = y + 1 - 2 * (y % 2)
    x_near = x + 1 - 2 * (x % 2)

    def device(xx, zz, yy, cc):
        return xx * 64 + zz * 8 + yy * 2 + cc

    core_peer = device(x, z, y, 1 - core)
    y_peer = device(x, z, y_near, core)
    x_peer = device(x_near, z, y, core)
    relay_peer = device(3 - x, z, y, core)
    plane = []
    for flip_x in range(2):
        for flip_y in range(2):
            for flip_core in range(2):
                if flip_x or flip_y or flip_core:
                    plane.append(
                        device(x_near if flip_x else x, z, y_near if flip_y else y, 1 - core if flip_core else core)
                    )

    half = y // 2
    rank = jnp.where(z < 4, z * 2 + half, 8 + half * 4 + 7 - z)

    def ranked(r):
        zz = jnp.where(r < 8, r // 2, 7 - r % 4)
        hh = jnp.where(r < 8, r % 2, (r - 8) // 4)
        return device(x, zz, jnp.where(hh == half, y, 3 - y), core)

    steps = range(1, 16)
    columns = {k: ranked((rank + k) % 16) for k in steps}

    def higher(k):
        return rank + k < 16

    remote_eight = (rank >= 8) & (rank < 11)

    def hears_later(k):
        return (rank == 7) & (k < 4)

    def fetch(src, dst, index):
        copy = pltpu.make_async_copy(src, dst, local_sem.at[index])
        copy.start()
        return copy

    get_features = fetch(features, raw, 0)
    get_row = fetch(virtual_states, virtual_row, 2)
    barrier = pltpu.get_barrier_semaphore()
    for k in steps:
        @pl.when(higher(k) & jnp.logical_not(hears_later(k)))
        def _(k=k):
            pl.semaphore_signal(barrier, inc=1, device_id=(columns[k],), device_id_type=MESH)
    for peer in plane:
        pl.semaphore_signal(barrier, inc=1, device_id=(peer,), device_id_type=MESH)
    @pl.when(x < 2)
    def _():
        pl.semaphore_signal(barrier, inc=1, device_id=(relay_peer,), device_id_type=MESH)

    get_gain = fetch(norm_gain, gain_ref, 1)
    get_query = fetch(w_query, wq, 3)
    get_key = fetch(key_weight, wkv.at[:, pl.ds(0, WIDTH)], 4)
    get_value = fetch(value_weight, wkv.at[:, pl.ds(WIDTH, WIDTH)], 5)
    get_pairs = fetch(block_pairs, pairs, 6)
    get_partners = fetch(partner_blocks, partners, 7)
    get_masks = fetch(masks, mask_raw, 8)

    def partner(m, b):
        return partners[m, b]

    group = z * 2 + y // 2
    member = x * 4 + (y % 2) * 2 + core
    get_row.wait()
    gather[group, pl.ds(member, 1)] = virtual_row[...].astype(F32)
    get_gain.wait()
    gain = gain_ref[...]
    get_features.wait()
    for block in range(BLOCKS):
        rows = pl.ds(block * BLK, BLK)
        normed[rows] = norm_rows(raw[rows].astype(F32), gain)

    def remote(src, dst, send, recv, peer):
        return pltpu.make_async_remote_copy(
            src_ref=src, dst_ref=dst, send_sem=send, recv_sem=recv, device_id=(peer,), device_id_type=MESH
        )

    def x_copy(r):
        c, part = r // PER_BLOCK, r % PER_BLOCK
        return remote(
            normed.at[pl.ds(r * RELAY, RELAY)],
            land.at[c, 1, pl.ds(part * RELAY, RELAY)],
            send_x.at[r], recv_x.at[r], x_peer,
        )

    def relay_copy(r):
        c, part = r // PER_BLOCK, r % PER_BLOCK
        return remote(
            land.at[c, 1, pl.ds(part * RELAY, RELAY)],
            land.at[c + 1, 2, pl.ds(part * RELAY, RELAY)],
            send_relay.at[r], recv_relay.at[r], relay_peer,
        )

    def y_copy(c):
        return remote(normed.at[pl.ds(c * BLK, BLK)], land.at[c, 0], send_y.at[c], recv_y.at[c], y_peer)

    copy_core = remote(normed, land_core, send_core.at[0], recv_core.at[0], core_peer)
    mine = gather.at[group, pl.ds(member, 1)]
    copy_plane = [remote(mine, mine, send_row.at[i], recv_row.at[i], peer) for i, peer in enumerate(plane)]
    eight = gather.at[group, pl.ds(pl.multiple_of(8 * (x // 2), 8), 8)]
    copy_across = remote(eight, eight, send_row.at[7], recv_row.at[7], relay_peer)
    sixteen = gather.at[group]

    def column_copy(k):
        return remote(sixteen, sixteen, send_row.at[7 + k], recv_row.at[7 + k], columns[k])

    def column_arrived(k):
        column_copy(16 - k).wait_recv()

    def tell_lower():
        @pl.when(x >= 2)
        def _():
            pl.semaphore_signal(entered.at[2], inc=1, device_id=(relay_peer,), device_id_type=MESH)
        @pl.when(rank == 11)
        def _():
            for k in (13, 14, 15):
                pl.semaphore_signal(token, inc=1, device_id=(columns[k],), device_id_type=MESH)
        for k in steps:
            @pl.when(jnp.logical_not(higher(k)) & jnp.logical_not(remote_eight & (rank + k == 16 + 7)))
            def _(k=k):
                crosses = jnp.where((rank >= 8) & (rank + k - 16 < 8), 1, 0)
                pl.semaphore_signal(entered.at[crosses], inc=1, device_id=(columns[k],), device_id_type=MESH)

    def tell_rank_seven():
        @pl.when(remote_eight)
        def _():
            pl.semaphore_wait(token, 1)
            seven = ranked(7)
            pl.semaphore_signal(entered.at[1], inc=1, device_id=(seven,), device_id_type=MESH)

    def send_lower():
        for k in steps:
            @pl.when(jnp.logical_not(higher(k)))
            def _(k=k):
                column_copy(k).start()

    def send_higher_near():
        @pl.when(rank % 8 < 7)
        def _():
            pl.semaphore_wait(entered.at[0], 7 - rank % 8)
        for k in range(1, 8):
            @pl.when(rank % 8 + k < 8)
            def _(k=k):
                column_copy(k).start()

    def send_higher_far():
        pl.semaphore_wait(entered.at[1], 8)
        for k in steps:
            @pl.when((rank + k >= 8) & higher(k))
            def _(k=k):
                column_copy(k).start()

    def send_bulk():
        for copy in copy_plane:
            copy.start()
        for c in range(BLOCKS):
            for part in range(PER_BLOCK):
                x_copy(c * PER_BLOCK + part).start()
            y_copy(c).start()
        copy_core.start()

    def relay(half_block):
        for part in range(BLK // 2 // RELAY):
            r = half_block * (BLK // 2 // RELAY) + part
            x_copy(r).wait_recv()
            relay_copy(r).start()

    even, odd = lane_halves(BLK)
    ones = jnp.concatenate([even, odd], axis=0)

    def widen(v2):
        return jnp.concatenate([v2, ones], axis=1)

    def project(rows, place_k, place_v, blocks):
        for offset, place in ((0, place_k), (WIDTH, place_v)):
            for jj in range(0, PAIR, 2):
                part = dot(rows, wkv[:, offset + jj * BLK:offset + (jj + 2) * BLK])
                for j in range(jj, jj + 2):
                    for b in range(blocks):
                        piece = part[b * BLK:(b + 1) * BLK, (j - jj) * BLK:(j - jj + 1) * BLK].astype(BF)
                        ref = place(b, j)
                        ref[0:BLK] = piece * even
                        ref[BLK:2 * BLK] = piece * odd

    def own_queries():
        get_query.wait()
        for jj in range(0, PAIR, 2):
            part = dot(normed[...], wq[:, jj * BLK:(jj + 2) * BLK]) * SCORE_SCALE
            for j in range(jj, jj + 2):
                for b in range(BLOCKS):
                    qs[j, b] = part[b * BLK:(b + 1) * BLK, (j - jj) * BLK:(j - jj + 1) * BLK].astype(BF)

    def own_keys_values():
        get_key.wait()
        get_value.wait()
        project(normed[...], lambda b, j: own_k.at[j, b], lambda b, j: own_v.at[j, b], BLOCKS)

    def spread_masks():
        get_masks.wait()
        get_pairs.wait()
        get_partners.wait()
        live = counts[0]
        for qb in range(BLOCKS):
            for kb in range(BLOCKS):
                slot = jnp.int32(0)
                for s in range(SLOTS):
                    slot = jnp.where((pairs[0, s] == qb) & (pairs[1, s] == kb), s, slot)
                alive = jnp.where(slot < live, 1, 0)
                keep[qb, kb] = (mask_raw[slot] * alive).astype(F32).astype(BF)

    def attend_local(pair_range):
        for j in pair_range:
            q = qs[j].reshape(ROWS, BLK)
            for kb in range(BLOCKS):
                s = scores(q, own_k[j, kb])
                for b in range(BLOCKS):
                    mask = keep[b, kb]
                    p = jnp.exp2(s[b * BLK:(b + 1) * BLK]).astype(BF)
                    weights[j, b * BLK:(b + 1) * BLK, kb * 2 * BLK:(kb + 1) * 2 * BLK] = p * jnp.concatenate(
                        [mask, mask], axis=1
                    )
        for j in pair_range:
            v = jnp.concatenate([widen(own_v[j, kb]) for kb in range(BLOCKS)], axis=0)
            near[j] = dot(weights[j], v).reshape(BLOCKS, BLK, 2 * BLK)

    def project_core():
        project(land_core[...], lambda b, j: core_k.at[b, j], lambda b, j: core_v.at[b, j], BLOCKS)

    def attend_core():
        block = [partner(0, b) for b in range(BLOCKS)]
        for j in range(PAIR):
            for b in range(BLOCKS):
                weights[j, b * BLK:(b + 1) * BLK, 0:2 * BLK] = jnp.exp2(
                    scores(qs[j, b], core_k[block[b], j])
                ).astype(BF)
        for j in range(PAIR):
            for b in range(BLOCKS):
                near[j, b] += dot(weights[j, b * BLK:(b + 1) * BLK, 0:2 * BLK], widen(core_v[block[b], j]))

    def far_step(c, sources):
        lo, hi = sources[0], sources[-1] + 1
        rows = land[c, lo:hi].reshape((hi - lo) * BLK, WIDTH)
        project(rows, lambda b, j: far_k.at[lo + b, j], lambda b, j: far_v.at[lo + b, j], hi - lo)
        for m in sources:
            block = c - 1 if m == 2 else c
            target = jnp.int32(0)
            for b in range(BLOCKS):
                target = jnp.where(partner(m + 1, b) == block, b, target)
            for j in range(PAIR):
                far_w[m, j] = jnp.exp2(scores(qs[j, target], far_k[m, j])).astype(BF)
        for m in sources:
            block = c - 1 if m == 2 else c
            for j in range(PAIR):
                far_acc[m, block, j] = dot(far_w[m, j], widen(far_v[m, j]))

    def arrive_relayed(c):
        for part in range(PER_BLOCK):
            relay_copy(c * PER_BLOCK + part).wait_recv()

    def virtual_nodes():
        even_v, odd_v = lane_halves(VIRTUAL)
        ones_v = jnp.concatenate([even_v, odd_v], axis=0)
        table = gather.reshape(256, BLK)
        state = jnp.concatenate([table[pl.ds(i, VIRTUAL, stride=4), :] for i in range(4)], axis=1)
        virtual_kv = dot(norm_rows(state, gain), wkv[...]).astype(BF)
        for j in range(PAIR):
            for offset, ref in ((0, virt_k), (WIDTH, virt_v)):
                piece = virtual_kv[:, offset + j * BLK:offset + (j + 1) * BLK]
                ref[j, 0:VIRTUAL] = piece * even_v
                ref[j, VIRTUAL:2 * VIRTUAL] = piece * odd_v
        for j in range(PAIR):
            s = scores(qs[j].reshape(ROWS, BLK), virt_k[j])
            weights[j, :, 0:BLK] = jnp.exp2(s).astype(BF)
        for j in range(PAIR):
            wide = jnp.concatenate([virt_v[j], ones_v], axis=1)
            near[j] += dot(weights[j, :, 0:BLK], wide).reshape(BLOCKS, BLK, 2 * BLK)

    def add_far():
        for j in range(PAIR):
            for b in range(BLOCKS):
                near[j, b] += far_acc[0, partner(1, b), j] + far_acc[1, partner(2, b), j]

    def finish():
        for b in range(BLOCKS):
            for j in range(PAIR):
                total = near[j, b] + far_acc[2, partner(3, b), j]
                out_ref[b * BLK:(b + 1) * BLK, j * BLK:(j + 1) * BLK] = (
                    total[:, 0:BLK] / total[:, BLK:2 * BLK]
                ).astype(BF)

    pl.semaphore_wait(barrier, 7 + x // 2 + rank - jnp.where(remote_eight, 1, 0))
    send_bulk()
    tell_lower()
    own_queries()
    own_keys_values()
    tell_rank_seven()
    spread_masks()
    attend_local((0, 1))
    for copy in copy_plane:
        copy.wait_recv()

    @pl.when(x < 2)
    def _():
        pl.semaphore_wait(entered.at[2], 1)
    copy_across.start()
    relay(0)
    attend_local((2, 3))
    relay(1)
    copy_core.wait_recv()
    project_core()
    copy_across.wait_recv()
    send_lower()
    relay(2)
    attend_core()
    send_higher_near()
    y_copy(0).wait_recv()
    far_step(0, (0, 1))
    relay(3)

    @pl.loop(1, BLOCKS)
    def _(c):
        @pl.when((z < 4) & (c == 2 - z // 2))
        def _():
            send_higher_far()

        y_copy(c).wait_recv()
        arrive_relayed(c - 1)
        far_step(c, (0, 1, 2))

        @pl.when(c < BLOCKS - 1)
        def _():
            relay(2 * c + 2)

        @pl.when(c == 3)
        def _():
            for k in steps:
                column_arrived(k)
            virtual_nodes()

        @pl.when(c < BLOCKS - 1)
        def _():
            relay(2 * c + 3)

    for copy in copy_plane + [copy_across, copy_core]:
        copy.wait_send()
    for r in range(RELAYS):
        x_copy(r).wait_send()
    for c in range(BLOCKS):
        y_copy(c).wait_send()
    add_far()
    for r in range(RELAYS - PER_BLOCK):
        relay_copy(r).wait_send()
    for k in steps:
        column_copy(k).wait_send()
    arrive_relayed(BLOCKS - 1)
    far_step(BLOCKS, (2,))
    finish()
    for r in range(RELAYS - PER_BLOCK, RELAYS):
        relay_copy(r).wait_send()


def local(
    features, norm_gain, w_query, key_weight, value_weight, w_out, virtual_states, block_pairs, block_masks,
    pair_counts, partners,
):
    dma = pltpu.SemaphoreType.DMA
    hbm = pl.BlockSpec(memory_space=pltpu.HBM)
    mixed = pl.pallas_call(
        kernel,
        out_shape=jax.ShapeDtypeStruct((ROWS, WIDTH), BF),
        in_specs=[hbm] * 8 + [pl.BlockSpec(memory_space=pltpu.SMEM), hbm],
        out_specs=pl.BlockSpec(memory_space=pltpu.VMEM),
        scratch_shapes=[
            pltpu.VMEM((1, WIDTH), F32),
            pltpu.VMEM((1, BLK), BF),
            pltpu.SMEM((2, SLOTS), jnp.int32),
            pltpu.SMEM((4, BLOCKS), jnp.int32),
            pltpu.VMEM((ROWS, WIDTH), BF),
            pltpu.VMEM((ROWS, WIDTH), BF),
            pltpu.VMEM((WIDTH, WIDTH), BF),
            pltpu.VMEM((WIDTH, 2 * WIDTH), BF),
            pltpu.VMEM((SLOTS, BLK, BLK), jnp.int32),
            pltpu.VMEM((BLOCKS, BLOCKS, BLK, BLK), BF),
            pltpu.VMEM((PAIR, BLOCKS, BLK, BLK), BF),
            pltpu.VMEM((PAIR, BLOCKS, 2 * BLK, BLK), BF),
            pltpu.VMEM((PAIR, BLOCKS, 2 * BLK, BLK), BF),
            pltpu.VMEM((ROWS, WIDTH), BF),
            pltpu.VMEM((BLOCKS, PAIR, 2 * BLK, BLK), BF),
            pltpu.VMEM((BLOCKS, PAIR, 2 * BLK, BLK), BF),
            pltpu.VMEM((BLOCKS + 1, 3, BLK, WIDTH), BF),
            pltpu.VMEM((3, PAIR, 2 * BLK, BLK), BF),
            pltpu.VMEM((3, PAIR, 2 * BLK, BLK), BF),
            pltpu.VMEM((PAIR, BLK, BLK), BF),
            pltpu.VMEM((PAIR, BLK, BLK), BF),
            pltpu.VMEM((16, 16, BLK), F32),
            pltpu.VMEM((PAIR, BLOCKS, BLK, 2 * BLK), F32),
            pltpu.VMEM((3, BLOCKS, PAIR, BLK, 2 * BLK), F32),
            pltpu.VMEM((PAIR, ROWS, 8 * BLK), BF),
            pltpu.VMEM((3, PAIR, BLK, 2 * BLK), BF),
            dma((9,)),
            dma((23,)), dma((23,)),
            dma((1,)), dma((1,)),
            dma((BLOCKS,)), dma((BLOCKS,)),
            dma((RELAYS,)), dma((RELAYS,)),
            dma((RELAYS,)), dma((RELAYS,)),
            pltpu.SemaphoreType.REGULAR((3,)),
            pltpu.SemaphoreType.REGULAR,
        ],
        compiler_params=pltpu.CompilerParams(
            collective_id=0, has_side_effects=True, vmem_limit_bytes=54500 * 1024
        ),
        cost_estimate=pl.CostEstimate(flops=8_000_000_000, bytes_accessed=4_500_000, transcendentals=4_500_000),
        name="expander_layer",
    )(
        features, norm_gain.reshape(1, WIDTH), w_query, key_weight, value_weight, virtual_states,
        block_pairs.T, block_masks, pair_counts, partners.reshape(4, BLOCKS),
    )
    return jnp.dot(mixed, w_out, preferred_element_type=F32).astype(BF)


def solution(mesh):
    placed = (
        P("nodes", None), P(), P(), P(), P(), P(), P("nodes", None), P("nodes", None), P("nodes", None, None),
        P("nodes"), P("nodes", None, None),
    )
    return jax.shard_map(local, mesh=mesh, in_specs=placed, out_specs=P("nodes", None), check_vma=False)
```

```python
import jax
import jax.numpy as jnp
from jax import lax
from jax.experimental import pallas as pl
from jax.experimental.pallas import tpu as pltpu
from jax.sharding import PartitionSpec as P

WIDTH = 512
HEAD = 64
BLK = 128
BLOCKS = 4
ROWS = BLK * BLOCKS
SLOTS = 16
VIRTUAL = 64
PAIR = 4
EPSILON = 1e-05
SCORE_SCALE = 1.4426950408889634 / 8.0
RELAY = 32
RELAYS = ROWS // RELAY
PER_BLOCK = BLK // RELAY
MESH = pl.DeviceIdType.MESH
BF = jnp.bfloat16
F32 = jnp.float32


def norm_rows(floats, gain):
    center = floats - jnp.mean(floats, axis=-1, keepdims=True)
    variance = jnp.mean(center * center, axis=-1, keepdims=True)
    return (center * lax.rsqrt(variance + EPSILON) * gain).astype(BF)


def scores(q, k2):
    return lax.dot_general(q, k2, (((1,), (1,)), ((), ())), preferred_element_type=F32) * SCORE_SCALE


def dot(a, b):
    return jnp.dot(a, b, preferred_element_type=F32)


def lane_halves(rows):
    lane = lax.broadcasted_iota(jnp.int32, (rows, BLK), 1)
    even = jnp.where(lane < HEAD, 1.0, 0.0).astype(BF)
    odd = jnp.where(lane < HEAD, 0.0, 1.0).astype(BF)
    return even, odd


def kernel(
    features, norm_gain, w_query, key_weight, value_weight, virtual_states, block_pairs, masks, counts, partner_blocks,
    out_ref,
    gain_ref, virtual_row, pairs, partners, raw, normed, wq, wkv, mask_raw, keep, qs, own_k, own_v, land_core, core_k,
    core_v, land, far_k, far_v, virt_k, virt_v, gather, near, far_acc, weights, far_w,
    local_sem, send_row, recv_row, send_core, recv_core, send_y, recv_y, send_x, recv_x, send_relay, recv_relay, entered, token,
):
    me = lax.axis_index("nodes")
    core = me % 2
    y = (me // 2) % 4
    z = (me // 8) % 8
    x = me // 64
    y_near = y + 1 - 2 * (y % 2)
    x_near = x + 1 - 2 * (x % 2)

    def device(xx, zz, yy, cc):
        return xx * 64 + zz * 8 + yy * 2 + cc

    core_peer = device(x, z, y, 1 - core)
    y_peer = device(x, z, y_near, core)
    x_peer = device(x_near, z, y, core)
    relay_peer = device(3 - x, z, y, core)
    plane = []
    for flip_x in range(2):
        for flip_y in range(2):
            for flip_core in range(2):
                if flip_x or flip_y or flip_core:
                    plane.append(
                        device(x_near if flip_x else x, z, y_near if flip_y else y, 1 - core if flip_core else core)
                    )

    half = y // 2
    rank = jnp.where(z < 4, z * 2 + half, 8 + half * 4 + 7 - z)

    def ranked(r):
        zz = jnp.where(r < 8, r // 2, 7 - r % 4)
        hh = jnp.where(r < 8, r % 2, (r - 8) // 4)
        return device(x, zz, jnp.where(hh == half, y, 3 - y), core)

    steps = range(1, 16)
    columns = {k: ranked((rank + k) % 16) for k in steps}

    def higher(k):
        return rank + k < 16

    remote_eight = (rank >= 8) & (rank < 11)

    def hears_later(k):
        return (rank == 7) & (k < 4)

    def fetch(src, dst, index):
        copy = pltpu.make_async_copy(src, dst, local_sem.at[index])
        copy.start()
        return copy

    get_features = fetch(features, raw, 0)
    get_row = fetch(virtual_states, virtual_row, 2)
    barrier = pltpu.get_barrier_semaphore()
    for peer in plane:
        pl.semaphore_signal(barrier, inc=1, device_id=(peer,), device_id_type=MESH)
    @pl.when(x < 2)
    def _():
        pl.semaphore_signal(barrier, inc=1, device_id=(relay_peer,), device_id_type=MESH)
    for k in steps:
        @pl.when(higher(k) & jnp.logical_not(hears_later(k)))
        def _(k=k):
            pl.semaphore_signal(barrier, inc=1, device_id=(columns[k],), device_id_type=MESH)

    get_gain = fetch(norm_gain, gain_ref, 1)
    group = z * 2 + y // 2
    member = x * 4 + (y % 2) * 2 + core
    get_row.wait()
    gather[group, pl.ds(member, 1)] = virtual_row[...].astype(F32)
    get_gain.wait()
    gain = gain_ref[...]
    get_features.wait()
    get_query = fetch(w_query, wq, 3)
    get_key = fetch(key_weight, wkv.at[:, pl.ds(0, WIDTH)], 4)
    get_value = fetch(value_weight, wkv.at[:, pl.ds(WIDTH, WIDTH)], 5)
    get_pairs = fetch(block_pairs, pairs, 6)
    get_partners = fetch(partner_blocks, partners, 7)
    get_masks = fetch(masks, mask_raw, 8)

    def partner(m, b):
        return partners[m, b]
    for block in range(BLOCKS):
        rows = pl.ds(block * BLK, BLK)
        normed[rows] = norm_rows(raw[rows].astype(F32), gain)

    def remote(src, dst, send, recv, peer):
        return pltpu.make_async_remote_copy(
            src_ref=src, dst_ref=dst, send_sem=send, recv_sem=recv, device_id=(peer,), device_id_type=MESH
        )

    def x_copy(r):
        c, part = r // PER_BLOCK, r % PER_BLOCK
        return remote(
            normed.at[pl.ds(r * RELAY, RELAY)],
            land.at[c, 1, pl.ds(part * RELAY, RELAY)],
            send_x.at[r], recv_x.at[r], x_peer,
        )

    def relay_copy(r):
        c, part = r // PER_BLOCK, r % PER_BLOCK
        return remote(
            land.at[c, 1, pl.ds(part * RELAY, RELAY)],
            land.at[c + 1, 2, pl.ds(part * RELAY, RELAY)],
            send_relay.at[r], recv_relay.at[r], relay_peer,
        )

    def y_copy(c):
        return remote(normed.at[pl.ds(c * BLK, BLK)], land.at[c, 0], send_y.at[c], recv_y.at[c], y_peer)

    copy_core = remote(normed, land_core, send_core.at[0], recv_core.at[0], core_peer)
    mine = gather.at[group, pl.ds(member, 1)]
    copy_plane = [remote(mine, mine, send_row.at[i], recv_row.at[i], peer) for i, peer in enumerate(plane)]
    eight = gather.at[group, pl.ds(pl.multiple_of(8 * (x // 2), 8), 8)]
    copy_across = remote(eight, eight, send_row.at[7], recv_row.at[7], relay_peer)
    sixteen = gather.at[group]

    def column_copy(k):
        return remote(sixteen, sixteen, send_row.at[7 + k], recv_row.at[7 + k], columns[k])

    def column_arrived(k):
        column_copy(16 - k).wait_recv()

    def tell_lower():
        @pl.when(x >= 2)
        def _():
            pl.semaphore_signal(entered.at[2], inc=1, device_id=(relay_peer,), device_id_type=MESH)
        @pl.when(rank == 11)
        def _():
            for k in (13, 14, 15):
                pl.semaphore_signal(token, inc=1, device_id=(columns[k],), device_id_type=MESH)
        for k in steps:
            @pl.when(jnp.logical_not(higher(k)) & jnp.logical_not(remote_eight & (rank + k == 16 + 7)))
            def _(k=k):
                crosses = jnp.where((rank >= 8) & (rank + k - 16 < 8), 1, 0)
                pl.semaphore_signal(entered.at[crosses], inc=1, device_id=(columns[k],), device_id_type=MESH)

    def tell_rank_seven():
        @pl.when(remote_eight)
        def _():
            pl.semaphore_wait(token, 1)
            seven = ranked(7)
            pl.semaphore_signal(entered.at[1], inc=1, device_id=(seven,), device_id_type=MESH)

    def send_lower():
        for k in steps:
            @pl.when(jnp.logical_not(higher(k)))
            def _(k=k):
                column_copy(k).start()

    def send_higher_near():
        @pl.when(rank % 8 < 7)
        def _():
            pl.semaphore_wait(entered.at[0], 7 - rank % 8)
        for k in range(1, 8):
            @pl.when(rank % 8 + k < 8)
            def _(k=k):
                column_copy(k).start()

    def send_higher_far():
        pl.semaphore_wait(entered.at[1], 8)
        for k in steps:
            @pl.when((rank + k >= 8) & higher(k))
            def _(k=k):
                column_copy(k).start()

    def send_bulk():
        x_copy(0).start()
        for copy in copy_plane:
            copy.start()
        for c in range(BLOCKS):
            for part in range(PER_BLOCK):
                if c or part:
                    x_copy(c * PER_BLOCK + part).start()
            y_copy(c).start()
        copy_core.start()

    def relay(half_block):
        for part in range(BLK // 2 // RELAY):
            r = half_block * (BLK // 2 // RELAY) + part
            x_copy(r).wait_recv()
            relay_copy(r).start()

    even, odd = lane_halves(BLK)
    ones = jnp.concatenate([even, odd], axis=0)

    def widen(v2):
        return jnp.concatenate([v2, ones], axis=1)

    def project(rows, place_k, place_v, blocks):
        for offset, place in ((0, place_k), (WIDTH, place_v)):
            for jj in range(0, PAIR, 2):
                part = dot(rows, wkv[:, offset + jj * BLK:offset + (jj + 2) * BLK])
                for j in range(jj, jj + 2):
                    for b in range(blocks):
                        piece = part[b * BLK:(b + 1) * BLK, (j - jj) * BLK:(j - jj + 1) * BLK].astype(BF)
                        ref = place(b, j)
                        ref[0:BLK] = piece * even
                        ref[BLK:2 * BLK] = piece * odd

    def own_queries():
        get_query.wait()
        for jj in range(0, PAIR, 2):
            part = dot(normed[...], wq[:, jj * BLK:(jj + 2) * BLK])
            for j in range(jj, jj + 2):
                for b in range(BLOCKS):
                    qs[j, b] = part[b * BLK:(b + 1) * BLK, (j - jj) * BLK:(j - jj + 1) * BLK].astype(BF)

    def own_keys_values():
        get_key.wait()
        get_value.wait()
        project(normed[...], lambda b, j: own_k.at[j, b], lambda b, j: own_v.at[j, b], BLOCKS)

    def spread_masks():
        get_masks.wait()
        get_pairs.wait()
        get_partners.wait()
        live = counts[0]
        for qb in range(BLOCKS):
            for kb in range(BLOCKS):
                slot = jnp.int32(0)
                for s in range(SLOTS):
                    slot = jnp.where((pairs[0, s] == qb) & (pairs[1, s] == kb), s, slot)
                alive = jnp.where(slot < live, 1, 0)
                keep[qb, kb] = (mask_raw[slot] * alive).astype(F32).astype(BF)

    def attend_local(pair_range):
        for j in pair_range:
            q = qs[j].reshape(ROWS, BLK)
            for kb in range(BLOCKS):
                s = scores(q, own_k[j, kb])
                for b in range(BLOCKS):
                    mask = keep[b, kb]
                    p = jnp.exp2(s[b * BLK:(b + 1) * BLK]).astype(BF)
                    weights[j, b * BLK:(b + 1) * BLK, kb * 2 * BLK:(kb + 1) * 2 * BLK] = p * jnp.concatenate(
                        [mask, mask], axis=1
                    )
        for j in pair_range:
            v = jnp.concatenate([widen(own_v[j, kb]) for kb in range(BLOCKS)], axis=0)
            near[j] = dot(weights[j], v).reshape(BLOCKS, BLK, 2 * BLK)

    def project_core():
        project(land_core[...], lambda b, j: core_k.at[b, j], lambda b, j: core_v.at[b, j], BLOCKS)

    def attend_core():
        block = [partner(0, b) for b in range(BLOCKS)]
        for j in range(PAIR):
            for b in range(BLOCKS):
                weights[j, b * BLK:(b + 1) * BLK, 0:2 * BLK] = jnp.exp2(
                    scores(qs[j, b], core_k[block[b], j])
                ).astype(BF)
        for j in range(PAIR):
            for b in range(BLOCKS):
                near[j, b] += dot(weights[j, b * BLK:(b + 1) * BLK, 0:2 * BLK], widen(core_v[block[b], j]))

    def far_step(c, sources):
        lo, hi = sources[0], sources[-1] + 1
        rows = land[c, lo:hi].reshape((hi - lo) * BLK, WIDTH)
        project(rows, lambda b, j: far_k.at[lo + b, j], lambda b, j: far_v.at[lo + b, j], hi - lo)
        for m in sources:
            block = c - 1 if m == 2 else c
            target = jnp.int32(0)
            for b in range(BLOCKS):
                target = jnp.where(partner(m + 1, b) == block, b, target)
            for j in range(PAIR):
                far_w[m, j] = jnp.exp2(scores(qs[j, target], far_k[m, j])).astype(BF)
        for m in sources:
            block = c - 1 if m == 2 else c
            for j in range(PAIR):
                far_acc[m, block, j] = dot(far_w[m, j], widen(far_v[m, j]))

    def arrive_relayed(c):
        for part in range(PER_BLOCK):
            relay_copy(c * PER_BLOCK + part).wait_recv()

    def virtual_nodes():
        even_v, odd_v = lane_halves(VIRTUAL)
        ones_v = jnp.concatenate([even_v, odd_v], axis=0)
        table = gather.reshape(256, BLK)
        state = jnp.concatenate([table[pl.ds(i, VIRTUAL, stride=4), :] for i in range(4)], axis=1)
        virtual_kv = dot(norm_rows(state, gain), wkv[...]).astype(BF)
        for j in range(PAIR):
            for offset, ref in ((0, virt_k), (WIDTH, virt_v)):
                piece = virtual_kv[:, offset + j * BLK:offset + (j + 1) * BLK]
                ref[j, 0:VIRTUAL] = piece * even_v
                ref[j, VIRTUAL:2 * VIRTUAL] = piece * odd_v
        for j in range(PAIR):
            s = scores(qs[j].reshape(ROWS, BLK), virt_k[j])
            weights[j, :, 0:BLK] = jnp.exp2(s).astype(BF)
        for j in range(PAIR):
            wide = jnp.concatenate([virt_v[j], ones_v], axis=1)
            near[j] += dot(weights[j, :, 0:BLK], wide).reshape(BLOCKS, BLK, 2 * BLK)

    def add_far():
        for j in range(PAIR):
            for b in range(BLOCKS):
                near[j, b] += far_acc[0, partner(1, b), j] + far_acc[1, partner(2, b), j]

    def finish():
        for b in range(BLOCKS):
            for j in range(PAIR):
                total = near[j, b] + far_acc[2, partner(3, b), j]
                out_ref[b * BLK:(b + 1) * BLK, j * BLK:(j + 1) * BLK] = (
                    total[:, 0:BLK] / total[:, BLK:2 * BLK]
                ).astype(BF)

    pl.semaphore_wait(barrier, 7 + x // 2 + rank - jnp.where(remote_eight, 1, 0))
    send_bulk()
    tell_lower()
    own_queries()
    own_keys_values()
    tell_rank_seven()
    spread_masks()
    attend_local((0, 1))
    for copy in copy_plane:
        copy.wait_recv()

    @pl.when(x < 2)
    def _():
        pl.semaphore_wait(entered.at[2], 1)
    copy_across.start()
    relay(0)
    attend_local((2, 3))
    relay(1)
    copy_core.wait_recv()
    project_core()
    copy_across.wait_recv()
    send_lower()
    relay(2)
    attend_core()
    send_higher_near()
    y_copy(0).wait_recv()
    far_step(0, (0, 1))
    relay(3)

    @pl.loop(1, BLOCKS)
    def _(c):
        @pl.when((z < 4) & (c == 2 - z // 2))
        def _():
            send_higher_far()

        y_copy(c).wait_recv()
        arrive_relayed(c - 1)
        far_step(c, (0, 1, 2))

        @pl.when(c < BLOCKS - 1)
        def _():
            relay(2 * c + 2)

        @pl.when(c == 3)
        def _():
            for k in steps:
                column_arrived(k)
            virtual_nodes()

        @pl.when(c < BLOCKS - 1)
        def _():
            relay(2 * c + 3)

    for copy in copy_plane + [copy_across, copy_core]:
        copy.wait_send()
    for r in range(RELAYS):
        x_copy(r).wait_send()
    for c in range(BLOCKS):
        y_copy(c).wait_send()
    add_far()
    for r in range(RELAYS - PER_BLOCK):
        relay_copy(r).wait_send()
    for k in steps:
        column_copy(k).wait_send()
    arrive_relayed(BLOCKS - 1)
    far_step(BLOCKS, (2,))
    finish()
    for r in range(RELAYS - PER_BLOCK, RELAYS):
        relay_copy(r).wait_send()


def out_kernel(mixed, w_ref, out_ref, rows, sems):
    copies = []
    for b in range(BLOCKS):
        part = pl.ds(b * BLK, BLK)
        rows[part] = dot(mixed[part], w_ref[...]).astype(BF)
        copies.append(pltpu.make_async_copy(rows.at[part], out_ref.at[part], sems.at[b]))
        copies[b].start()
    for copy in copies:
        copy.wait()


def local(
    features, norm_gain, w_query, key_weight, value_weight, w_out, virtual_states, block_pairs, block_masks,
    pair_counts, partners,
):
    dma = pltpu.SemaphoreType.DMA
    hbm = pl.BlockSpec(memory_space=pltpu.HBM)
    mixed = pl.pallas_call(
        kernel,
        out_shape=jax.ShapeDtypeStruct((ROWS, WIDTH), BF),
        in_specs=[hbm] * 8 + [pl.BlockSpec(memory_space=pltpu.SMEM), hbm],
        out_specs=pl.BlockSpec(memory_space=pltpu.VMEM),
        scratch_shapes=[
            pltpu.VMEM((1, WIDTH), F32),
            pltpu.VMEM((1, BLK), BF),
            pltpu.SMEM((2, SLOTS), jnp.int32),
            pltpu.SMEM((4, BLOCKS), jnp.int32),
            pltpu.VMEM((ROWS, WIDTH), BF),
            pltpu.VMEM((ROWS, WIDTH), BF),
            pltpu.VMEM((WIDTH, WIDTH), BF),
            pltpu.VMEM((WIDTH, 2 * WIDTH), BF),
            pltpu.VMEM((SLOTS, BLK, BLK), jnp.int32),
            pltpu.VMEM((BLOCKS, BLOCKS, BLK, BLK), BF),
            pltpu.VMEM((PAIR, BLOCKS, BLK, BLK), BF),
            pltpu.VMEM((PAIR, BLOCKS, 2 * BLK, BLK), BF),
            pltpu.VMEM((PAIR, BLOCKS, 2 * BLK, BLK), BF),
            pltpu.VMEM((ROWS, WIDTH), BF),
            pltpu.VMEM((BLOCKS, PAIR, 2 * BLK, BLK), BF),
            pltpu.VMEM((BLOCKS, PAIR, 2 * BLK, BLK), BF),
            pltpu.VMEM((BLOCKS + 1, 3, BLK, WIDTH), BF),
            pltpu.VMEM((3, PAIR, 2 * BLK, BLK), BF),
            pltpu.VMEM((3, PAIR, 2 * BLK, BLK), BF),
            pltpu.VMEM((PAIR, BLK, BLK), BF),
            pltpu.VMEM((PAIR, BLK, BLK), BF),
            pltpu.VMEM((16, 16, BLK), F32),
            pltpu.VMEM((PAIR, BLOCKS, BLK, 2 * BLK), F32),
            pltpu.VMEM((3, BLOCKS, PAIR, BLK, 2 * BLK), F32),
            pltpu.VMEM((PAIR, ROWS, 8 * BLK), BF),
            pltpu.VMEM((3, PAIR, BLK, 2 * BLK), BF),
            dma((9,)),
            dma((23,)), dma((23,)),
            dma((1,)), dma((1,)),
            dma((BLOCKS,)), dma((BLOCKS,)),
            dma((RELAYS,)), dma((RELAYS,)),
            dma((RELAYS,)), dma((RELAYS,)),
            pltpu.SemaphoreType.REGULAR((3,)),
            pltpu.SemaphoreType.REGULAR,
        ],
        compiler_params=pltpu.CompilerParams(
            collective_id=0, has_side_effects=True, vmem_limit_bytes=54500 * 1024
        ),
        cost_estimate=pl.CostEstimate(flops=8_000_000_000, bytes_accessed=4_500_000, transcendentals=4_500_000),
        name="expander_layer",
    )(
        *(
            pltpu.with_memory_space_constraint(a, pltpu.HBM)
            for a in (
                features, norm_gain.reshape(1, WIDTH), w_query, key_weight, value_weight, virtual_states,
                block_pairs.T, block_masks,
            )
        ),
        pair_counts,
        pltpu.with_memory_space_constraint(partners.reshape(4, BLOCKS), pltpu.HBM),
    )
    vmem = pl.BlockSpec(memory_space=pltpu.VMEM)
    return pl.pallas_call(
        out_kernel,
        out_shape=jax.ShapeDtypeStruct((ROWS, WIDTH), BF),
        in_specs=[vmem, vmem],
        out_specs=hbm,
        scratch_shapes=[pltpu.VMEM((ROWS, WIDTH), BF), dma((BLOCKS,))],
        compiler_params=pltpu.CompilerParams(vmem_limit_bytes=8 * 1024 * 1024),
        cost_estimate=pl.CostEstimate(flops=270_000_000, bytes_accessed=1_600_000, transcendentals=0),
        name="out_projection",
    )(mixed, w_out)


def solution(mesh):
    placed = (
        P("nodes", None), P(), P(), P(), P(), P(), P("nodes", None), P("nodes", None), P("nodes", None, None),
        P("nodes"), P("nodes", None, None),
    )
    return jax.shard_map(local, mesh=mesh, in_specs=placed, out_specs=P("nodes", None), check_vma=False)
```

```python
import jax
import jax.numpy as jnp
from jax import lax
from jax.experimental import pallas as pl
from jax.experimental.pallas import tpu as pltpu
from jax.sharding import PartitionSpec as P

WIDTH = 512
HEAD = 64
BLK = 128
BLOCKS = 4
ROWS = BLK * BLOCKS
SLOTS = 16
VIRTUAL = 64
PAIR = 4
EPSILON = 1e-05
SCORE_SCALE = 1.4426950408889634 / 8.0
RELAY = 32
RELAYS = ROWS // RELAY
PER_BLOCK = BLK // RELAY
MESH = pl.DeviceIdType.MESH
BF = jnp.bfloat16
F32 = jnp.float32


def norm_rows(floats, gain):
    center = floats - jnp.mean(floats, axis=-1, keepdims=True)
    variance = jnp.mean(center * center, axis=-1, keepdims=True)
    return (center * lax.rsqrt(variance + EPSILON) * gain).astype(BF)


def scores(q, k2):
    return lax.dot_general(q, k2, (((1,), (1,)), ((), ())), preferred_element_type=F32) * SCORE_SCALE


def dot(a, b):
    return jnp.dot(a, b, preferred_element_type=F32)


def lane_halves(rows):
    lane = lax.broadcasted_iota(jnp.int32, (rows, BLK), 1)
    even = jnp.where(lane < HEAD, 1.0, 0.0).astype(BF)
    odd = jnp.where(lane < HEAD, 0.0, 1.0).astype(BF)
    return even, odd


def kernel(
    features, norm_gain, w_query, key_weight, value_weight, virtual_states, block_pairs, masks, counts, partner_blocks,
    out_ref,
    gain_ref, virtual_row, pairs, partners, raw, normed, wq, wkv, mask_raw, keep, qs, own_k, own_v, land_core, core_k,
    core_v, land, far_k, far_v, virt_k, virt_v, gather, near, far_acc, weights, far_w,
    local_sem, send_row, recv_row, send_core, recv_core, send_y, recv_y, send_x, recv_x, send_relay, recv_relay, entered, token,
):
    me = lax.axis_index("nodes")
    core = me % 2
    y = (me // 2) % 4
    z = (me // 8) % 8
    x = me // 64
    y_near = y + 1 - 2 * (y % 2)
    x_near = x + 1 - 2 * (x % 2)

    def device(xx, zz, yy, cc):
        return xx * 64 + zz * 8 + yy * 2 + cc

    core_peer = device(x, z, y, 1 - core)
    y_peer = device(x, z, y_near, core)
    x_peer = device(x_near, z, y, core)
    relay_peer = device(3 - x, z, y, core)
    plane = []
    for flip_x in range(2):
        for flip_y in range(2):
            for flip_core in range(2):
                if flip_x or flip_y or flip_core:
                    plane.append(
                        device(x_near if flip_x else x, z, y_near if flip_y else y, 1 - core if flip_core else core)
                    )

    half = y // 2
    rank = jnp.where(z < 4, z * 2 + half, 8 + half * 4 + 7 - z)

    def ranked(r):
        zz = jnp.where(r < 8, r // 2, 7 - r % 4)
        hh = jnp.where(r < 8, r % 2, (r - 8) // 4)
        return device(x, zz, jnp.where(hh == half, y, 3 - y), core)

    steps = range(1, 16)
    columns = {k: ranked((rank + k) % 16) for k in steps}

    def higher(k):
        return rank + k < 16

    remote_eight = (rank >= 8) & (rank < 11)

    def hears_later(k):
        return (rank == 7) & (k < 4)

    def fetch(src, dst, index):
        copy = pltpu.make_async_copy(src, dst, local_sem.at[index])
        copy.start()
        return copy

    get_features = fetch(features, raw, 0)
    get_row = fetch(virtual_states, virtual_row, 2)
    barrier = pltpu.get_barrier_semaphore()
    for peer in plane:
        pl.semaphore_signal(barrier, inc=1, device_id=(peer,), device_id_type=MESH)
    @pl.when(x < 2)
    def _():
        pl.semaphore_signal(barrier, inc=1, device_id=(relay_peer,), device_id_type=MESH)
    for k in steps:
        @pl.when(higher(k) & jnp.logical_not(hears_later(k)))
        def _(k=k):
            pl.semaphore_signal(barrier, inc=1, device_id=(columns[k],), device_id_type=MESH)

    get_gain = fetch(norm_gain, gain_ref, 1)
    group = z * 2 + y // 2
    member = x * 4 + (y % 2) * 2 + core
    get_row.wait()
    gather[group, pl.ds(member, 1)] = virtual_row[...].astype(F32)
    get_gain.wait()
    gain = gain_ref[...]
    get_features.wait()
    get_query = fetch(w_query, wq, 3)
    get_key = fetch(key_weight, wkv.at[:, pl.ds(0, WIDTH)], 4)
    get_value = fetch(value_weight, wkv.at[:, pl.ds(WIDTH, WIDTH)], 5)
    get_pairs = fetch(block_pairs, pairs, 6)
    get_partners = fetch(partner_blocks, partners, 7)
    get_masks = fetch(masks, mask_raw, 8)

    def partner(m, b):
        return partners[m, b]
    for block in range(BLOCKS):
        rows = pl.ds(block * BLK, BLK)
        normed[rows] = norm_rows(raw[rows].astype(F32), gain)

    def remote(src, dst, send, recv, peer):
        return pltpu.make_async_remote_copy(
            src_ref=src, dst_ref=dst, send_sem=send, recv_sem=recv, device_id=(peer,), device_id_type=MESH
        )

    def x_copy(r):
        c, part = r // PER_BLOCK, r % PER_BLOCK
        return remote(
            normed.at[pl.ds(r * RELAY, RELAY)],
            land.at[c, 1, pl.ds(part * RELAY, RELAY)],
            send_x.at[r], recv_x.at[r], x_peer,
        )

    def relay_copy(r):
        c, part = r // PER_BLOCK, r % PER_BLOCK
        return remote(
            land.at[c, 1, pl.ds(part * RELAY, RELAY)],
            land.at[c + 1, 2, pl.ds(part * RELAY, RELAY)],
            send_relay.at[r], recv_relay.at[r], relay_peer,
        )

    def y_copy(c):
        return remote(normed.at[pl.ds(c * BLK, BLK)], land.at[c, 0], send_y.at[c], recv_y.at[c], y_peer)

    copy_core = remote(normed, land_core, send_core.at[0], recv_core.at[0], core_peer)
    mine = gather.at[group, pl.ds(member, 1)]
    copy_plane = [remote(mine, mine, send_row.at[i], recv_row.at[i], peer) for i, peer in enumerate(plane)]
    eight = gather.at[group, pl.ds(pl.multiple_of(8 * (x // 2), 8), 8)]
    copy_across = remote(eight, eight, send_row.at[7], recv_row.at[7], relay_peer)
    sixteen = gather.at[group]

    def column_copy(k):
        return remote(sixteen, sixteen, send_row.at[7 + k], recv_row.at[7 + k], columns[k])

    def column_arrived(k):
        column_copy(16 - k).wait_recv()

    def tell_lower():
        @pl.when(x >= 2)
        def _():
            pl.semaphore_signal(entered.at[2], inc=1, device_id=(relay_peer,), device_id_type=MESH)
        @pl.when(rank == 11)
        def _():
            for k in (13, 14, 15):
                pl.semaphore_signal(token, inc=1, device_id=(columns[k],), device_id_type=MESH)
        for k in steps:
            @pl.when(jnp.logical_not(higher(k)) & jnp.logical_not(remote_eight & (rank + k == 16 + 7)))
            def _(k=k):
                crosses = jnp.where((rank >= 8) & (rank + k - 16 < 8), 1, 0)
                pl.semaphore_signal(entered.at[crosses], inc=1, device_id=(columns[k],), device_id_type=MESH)

    def tell_rank_seven():
        @pl.when(remote_eight)
        def _():
            pl.semaphore_wait(token, 1)
            seven = ranked(7)
            pl.semaphore_signal(entered.at[1], inc=1, device_id=(seven,), device_id_type=MESH)

    def send_lower():
        for k in steps:
            @pl.when(jnp.logical_not(higher(k)))
            def _(k=k):
                column_copy(k).start()

    def send_higher_near():
        @pl.when(rank % 8 < 7)
        def _():
            pl.semaphore_wait(entered.at[0], 7 - rank % 8)
        for k in range(1, 8):
            @pl.when(rank % 8 + k < 8)
            def _(k=k):
                column_copy(k).start()

    def send_higher_far():
        pl.semaphore_wait(entered.at[1], 8)
        for k in steps:
            @pl.when((rank + k >= 8) & higher(k))
            def _(k=k):
                column_copy(k).start()

    def send_bulk():
        x_copy(0).start()
        for copy in copy_plane:
            copy.start()
        for c in range(BLOCKS):
            for part in range(PER_BLOCK):
                if c or part:
                    x_copy(c * PER_BLOCK + part).start()
            y_copy(c).start()
        copy_core.start()

    def relay(half_block):
        for part in range(BLK // 2 // RELAY):
            r = half_block * (BLK // 2 // RELAY) + part
            x_copy(r).wait_recv()
            relay_copy(r).start()

    even, odd = lane_halves(BLK)
    ones = jnp.concatenate([even, odd], axis=0)

    def widen(v2):
        return jnp.concatenate([v2, ones], axis=1)

    def project(rows, place_k, place_v, blocks):
        for offset, place in ((0, place_k), (WIDTH, place_v)):
            for jj in range(0, PAIR, 2):
                part = dot(rows, wkv[:, offset + jj * BLK:offset + (jj + 2) * BLK])
                for j in range(jj, jj + 2):
                    for b in range(blocks):
                        piece = part[b * BLK:(b + 1) * BLK, (j - jj) * BLK:(j - jj + 1) * BLK].astype(BF)
                        ref = place(b, j)
                        ref[0:BLK] = piece * even
                        ref[BLK:2 * BLK] = piece * odd

    def own_queries():
        get_query.wait()
        for jj in range(0, PAIR, 2):
            part = dot(normed[...], wq[:, jj * BLK:(jj + 2) * BLK])
            for j in range(jj, jj + 2):
                for b in range(BLOCKS):
                    qs[j, b] = part[b * BLK:(b + 1) * BLK, (j - jj) * BLK:(j - jj + 1) * BLK].astype(BF)

    def own_keys_values():
        get_key.wait()
        get_value.wait()
        project(normed[...], lambda b, j: own_k.at[j, b], lambda b, j: own_v.at[j, b], BLOCKS)

    def spread_masks():
        get_masks.wait()
        get_pairs.wait()
        get_partners.wait()
        live = counts[0]
        for qb in range(BLOCKS):
            for kb in range(BLOCKS):
                slot = jnp.int32(0)
                for s in range(SLOTS):
                    slot = jnp.where((pairs[0, s] == qb) & (pairs[1, s] == kb), s, slot)
                alive = jnp.where(slot < live, 1, 0)
                keep[qb, kb] = (mask_raw[slot] * alive).astype(F32).astype(BF)

    def attend_local(pair_range):
        for j in pair_range:
            q = qs[j].reshape(ROWS, BLK)
            for kb in range(BLOCKS):
                s = scores(q, own_k[j, kb])
                for b in range(BLOCKS):
                    mask = keep[b, kb]
                    p = jnp.exp2(s[b * BLK:(b + 1) * BLK]).astype(BF)
                    weights[j, b * BLK:(b + 1) * BLK, kb * 2 * BLK:(kb + 1) * 2 * BLK] = p * jnp.concatenate(
                        [mask, mask], axis=1
                    )
        for j in pair_range:
            v = jnp.concatenate([widen(own_v[j, kb]) for kb in range(BLOCKS)], axis=0)
            near[j] = dot(weights[j], v).reshape(BLOCKS, BLK, 2 * BLK)

    def project_core():
        project(land_core[...], lambda b, j: core_k.at[b, j], lambda b, j: core_v.at[b, j], BLOCKS)

    def attend_core():
        block = [partner(0, b) for b in range(BLOCKS)]
        for j in range(PAIR):
            for b in range(BLOCKS):
                weights[j, b * BLK:(b + 1) * BLK, 0:2 * BLK] = jnp.exp2(
                    scores(qs[j, b], core_k[block[b], j])
                ).astype(BF)
        for j in range(PAIR):
            for b in range(BLOCKS):
                near[j, b] += dot(weights[j, b * BLK:(b + 1) * BLK, 0:2 * BLK], widen(core_v[block[b], j]))

    def far_step(c, sources):
        lo, hi = sources[0], sources[-1] + 1
        rows = land[c, lo:hi].reshape((hi - lo) * BLK, WIDTH)
        project(rows, lambda b, j: far_k.at[lo + b, j], lambda b, j: far_v.at[lo + b, j], hi - lo)
        for m in sources:
            block = c - 1 if m == 2 else c
            target = jnp.int32(0)
            for b in range(BLOCKS):
                target = jnp.where(partner(m + 1, b) == block, b, target)
            for j in range(PAIR):
                far_w[m, j] = jnp.exp2(scores(qs[j, target], far_k[m, j])).astype(BF)
        for m in sources:
            block = c - 1 if m == 2 else c
            for j in range(PAIR):
                far_acc[m, block, j] = dot(far_w[m, j], widen(far_v[m, j]))

    def arrive_relayed(c):
        for part in range(PER_BLOCK):
            relay_copy(c * PER_BLOCK + part).wait_recv()

    def virtual_nodes():
        even_v, odd_v = lane_halves(VIRTUAL)
        ones_v = jnp.concatenate([even_v, odd_v], axis=0)
        table = gather.reshape(256, BLK)
        state = jnp.concatenate([table[pl.ds(i, VIRTUAL, stride=4), :] for i in range(4)], axis=1)
        virtual_kv = dot(norm_rows(state, gain), wkv[...]).astype(BF)
        for j in range(PAIR):
            for offset, ref in ((0, virt_k), (WIDTH, virt_v)):
                piece = virtual_kv[:, offset + j * BLK:offset + (j + 1) * BLK]
                ref[j, 0:VIRTUAL] = piece * even_v
                ref[j, VIRTUAL:2 * VIRTUAL] = piece * odd_v
        for j in range(PAIR):
            s = scores(qs[j].reshape(ROWS, BLK), virt_k[j])
            weights[j, :, 0:BLK] = jnp.exp2(s).astype(BF)
        for j in range(PAIR):
            wide = jnp.concatenate([virt_v[j], ones_v], axis=1)
            near[j] += dot(weights[j, :, 0:BLK], wide).reshape(BLOCKS, BLK, 2 * BLK)

    def add_far():
        for j in range(PAIR):
            for b in range(BLOCKS):
                near[j, b] += far_acc[0, partner(1, b), j] + far_acc[1, partner(2, b), j]

    def finish():
        for b in range(BLOCKS):
            for j in range(PAIR):
                total = near[j, b] + far_acc[2, partner(3, b), j]
                out_ref[b * BLK:(b + 1) * BLK, j * BLK:(j + 1) * BLK] = (
                    total[:, 0:BLK] / total[:, BLK:2 * BLK]
                ).astype(BF)

    pl.semaphore_wait(barrier, 7 + x // 2 + rank - jnp.where(remote_eight, 1, 0))
    send_bulk()
    tell_lower()
    own_queries()
    own_keys_values()
    tell_rank_seven()
    spread_masks()
    attend_local((0, 1))
    for copy in copy_plane:
        copy.wait_recv()

    @pl.when(x < 2)
    def _():
        pl.semaphore_wait(entered.at[2], 1)
    copy_across.start()
    relay(0)
    attend_local((2, 3))
    relay(1)
    copy_core.wait_recv()
    project_core()
    copy_across.wait_recv()
    send_lower()
    relay(2)
    attend_core()
    send_higher_near()
    y_copy(0).wait_recv()
    far_step(0, (0, 1))
    relay(3)

    @pl.loop(1, BLOCKS)
    def _(c):
        @pl.when((z < 4) & (c == 2 - z // 2))
        def _():
            send_higher_far()

        y_copy(c).wait_recv()
        far_step(c, (0, 1))

        @pl.when(c < BLOCKS - 1)
        def _():
            relay(2 * c + 2)

        arrive_relayed(c - 1)
        far_step(c, (2,))

        @pl.when(c == 3)
        def _():
            for k in steps:
                column_arrived(k)
            virtual_nodes()

        @pl.when(c < BLOCKS - 1)
        def _():
            relay(2 * c + 3)

    for copy in copy_plane + [copy_across, copy_core]:
        copy.wait_send()
    for r in range(RELAYS):
        x_copy(r).wait_send()
    for c in range(BLOCKS):
        y_copy(c).wait_send()
    add_far()
    for r in range(RELAYS - PER_BLOCK):
        relay_copy(r).wait_send()
    for k in steps:
        column_copy(k).wait_send()
    arrive_relayed(BLOCKS - 1)
    far_step(BLOCKS, (2,))
    finish()
    for r in range(RELAYS - PER_BLOCK, RELAYS):
        relay_copy(r).wait_send()


def out_kernel(mixed, w_ref, out_ref, rows, sems):
    copies = []
    for b in range(BLOCKS):
        part = pl.ds(b * BLK, BLK)
        rows[part] = dot(mixed[part], w_ref[...]).astype(BF)
        copies.append(pltpu.make_async_copy(rows.at[part], out_ref.at[part], sems.at[b]))
        copies[b].start()
    for copy in copies:
        copy.wait()


def local(
    features, norm_gain, w_query, key_weight, value_weight, w_out, virtual_states, block_pairs, block_masks,
    pair_counts, partners,
):
    dma = pltpu.SemaphoreType.DMA
    hbm = pl.BlockSpec(memory_space=pltpu.HBM)
    mixed = pl.pallas_call(
        kernel,
        out_shape=jax.ShapeDtypeStruct((ROWS, WIDTH), BF),
        in_specs=[hbm] * 8 + [pl.BlockSpec(memory_space=pltpu.SMEM), hbm],
        out_specs=pl.BlockSpec(memory_space=pltpu.VMEM),
        scratch_shapes=[
            pltpu.VMEM((1, WIDTH), F32),
            pltpu.VMEM((1, BLK), BF),
            pltpu.SMEM((2, SLOTS), jnp.int32),
            pltpu.SMEM((4, BLOCKS), jnp.int32),
            pltpu.VMEM((ROWS, WIDTH), BF),
            pltpu.VMEM((ROWS, WIDTH), BF),
            pltpu.VMEM((WIDTH, WIDTH), BF),
            pltpu.VMEM((WIDTH, 2 * WIDTH), BF),
            pltpu.VMEM((SLOTS, BLK, BLK), jnp.int32),
            pltpu.VMEM((BLOCKS, BLOCKS, BLK, BLK), BF),
            pltpu.VMEM((PAIR, BLOCKS, BLK, BLK), BF),
            pltpu.VMEM((PAIR, BLOCKS, 2 * BLK, BLK), BF),
            pltpu.VMEM((PAIR, BLOCKS, 2 * BLK, BLK), BF),
            pltpu.VMEM((ROWS, WIDTH), BF),
            pltpu.VMEM((BLOCKS, PAIR, 2 * BLK, BLK), BF),
            pltpu.VMEM((BLOCKS, PAIR, 2 * BLK, BLK), BF),
            pltpu.VMEM((BLOCKS + 1, 3, BLK, WIDTH), BF),
            pltpu.VMEM((3, PAIR, 2 * BLK, BLK), BF),
            pltpu.VMEM((3, PAIR, 2 * BLK, BLK), BF),
            pltpu.VMEM((PAIR, BLK, BLK), BF),
            pltpu.VMEM((PAIR, BLK, BLK), BF),
            pltpu.VMEM((16, 16, BLK), F32),
            pltpu.VMEM((PAIR, BLOCKS, BLK, 2 * BLK), F32),
            pltpu.VMEM((3, BLOCKS, PAIR, BLK, 2 * BLK), F32),
            pltpu.VMEM((PAIR, ROWS, 8 * BLK), BF),
            pltpu.VMEM((3, PAIR, BLK, 2 * BLK), BF),
            dma((9,)),
            dma((23,)), dma((23,)),
            dma((1,)), dma((1,)),
            dma((BLOCKS,)), dma((BLOCKS,)),
            dma((RELAYS,)), dma((RELAYS,)),
            dma((RELAYS,)), dma((RELAYS,)),
            pltpu.SemaphoreType.REGULAR((3,)),
            pltpu.SemaphoreType.REGULAR,
        ],
        compiler_params=pltpu.CompilerParams(
            collective_id=0, has_side_effects=True, vmem_limit_bytes=54500 * 1024
        ),
        cost_estimate=pl.CostEstimate(flops=8_000_000_000, bytes_accessed=4_500_000, transcendentals=4_500_000),
        name="expander_layer",
    )(
        *(
            pltpu.with_memory_space_constraint(a, pltpu.HBM)
            for a in (
                features, norm_gain.reshape(1, WIDTH), w_query, key_weight, value_weight, virtual_states,
                block_pairs.T, block_masks,
            )
        ),
        pair_counts,
        pltpu.with_memory_space_constraint(partners.reshape(4, BLOCKS), pltpu.HBM),
    )
    vmem = pl.BlockSpec(memory_space=pltpu.VMEM)
    return pl.pallas_call(
        out_kernel,
        out_shape=jax.ShapeDtypeStruct((ROWS, WIDTH), BF),
        in_specs=[vmem, vmem],
        out_specs=hbm,
        scratch_shapes=[pltpu.VMEM((ROWS, WIDTH), BF), dma((BLOCKS,))],
        compiler_params=pltpu.CompilerParams(vmem_limit_bytes=8 * 1024 * 1024),
        cost_estimate=pl.CostEstimate(flops=270_000_000, bytes_accessed=1_600_000, transcendentals=0),
        name="out_projection",
    )(mixed, w_out)


def solution(mesh):
    placed = (
        P("nodes", None), P(), P(), P(), P(), P(), P("nodes", None), P("nodes", None), P("nodes", None, None),
        P("nodes"), P("nodes", None, None),
    )
    return jax.shard_map(local, mesh=mesh, in_specs=placed, out_specs=P("nodes", None), check_vma=False)
```

```python
import jax
import jax.numpy as jnp
from jax import lax
from jax.experimental import pallas as pl
from jax.experimental.pallas import tpu as pltpu
from jax.sharding import PartitionSpec as P

WIDTH = 512
HEAD = 64
BLK = 128
BLOCKS = 4
ROWS = BLK * BLOCKS
SLOTS = 16
VIRTUAL = 64
PAIR = 4
EPSILON = 1e-05
SCORE_SCALE = 1.4426950408889634 / 8.0
RELAY = 32
RELAYS = ROWS // RELAY
PER_BLOCK = BLK // RELAY
MESH = pl.DeviceIdType.MESH
BF = jnp.bfloat16
F32 = jnp.float32


def norm_rows(floats, gain):
    center = floats - jnp.mean(floats, axis=-1, keepdims=True)
    variance = jnp.mean(center * center, axis=-1, keepdims=True)
    return (center * lax.rsqrt(variance + EPSILON) * gain).astype(BF)


def scores(q, k2):
    return lax.dot_general(q, k2, (((1,), (1,)), ((), ())), preferred_element_type=F32) * SCORE_SCALE


def dot(a, b):
    return jnp.dot(a, b, preferred_element_type=F32)


def lane_halves(rows):
    lane = lax.broadcasted_iota(jnp.int32, (rows, BLK), 1)
    even = jnp.where(lane < HEAD, 1.0, 0.0).astype(BF)
    odd = jnp.where(lane < HEAD, 0.0, 1.0).astype(BF)
    return even, odd


def kernel(
    features, norm_gain, w_query, key_weight, value_weight, virtual_states, block_pairs, masks, counts, partner_blocks,
    out_ref,
    gain_ref, virtual_row, pairs, partners, raw, normed, wq, wkv, mask_raw, keep, qs, own_k, own_v, land_core, core_k,
    core_v, land, far_k, far_v, virt_k, virt_v, gather, near, far_acc, weights, far_w,
    local_sem, send_row, recv_row, send_core, recv_core, send_y, recv_y, send_x, recv_x, send_relay, recv_relay, entered, token,
):
    me = lax.axis_index("nodes")
    core = me % 2
    y = (me // 2) % 4
    z = (me // 8) % 8
    x = me // 64
    y_near = y + 1 - 2 * (y % 2)
    x_near = x + 1 - 2 * (x % 2)

    def device(xx, zz, yy, cc):
        return xx * 64 + zz * 8 + yy * 2 + cc

    core_peer = device(x, z, y, 1 - core)
    y_peer = device(x, z, y_near, core)
    x_peer = device(x_near, z, y, core)
    relay_peer = device(3 - x, z, y, core)
    plane = []
    for flip_x in range(2):
        for flip_y in range(2):
            for flip_core in range(2):
                if flip_x or flip_y or flip_core:
                    plane.append(
                        device(x_near if flip_x else x, z, y_near if flip_y else y, 1 - core if flip_core else core)
                    )

    half = y // 2
    rank = jnp.where(z < 4, z * 2 + half, 8 + half * 4 + 7 - z)

    def ranked(r):
        zz = jnp.where(r < 8, r // 2, 7 - r % 4)
        hh = jnp.where(r < 8, r % 2, (r - 8) // 4)
        return device(x, zz, jnp.where(hh == half, y, 3 - y), core)

    steps = range(1, 16)
    columns = {k: ranked((rank + k) % 16) for k in steps}

    def higher(k):
        return rank + k < 16

    remote_eight = (rank >= 8) & (rank < 11)

    def hears_later(k):
        return (rank == 7) & (k < 4)

    def fetch(src, dst, index):
        copy = pltpu.make_async_copy(src, dst, local_sem.at[index])
        copy.start()
        return copy

    get_features = fetch(features, raw, 0)
    get_row = fetch(virtual_states, virtual_row, 2)
    barrier = pltpu.get_barrier_semaphore()
    for peer in plane:
        pl.semaphore_signal(barrier, inc=1, device_id=(peer,), device_id_type=MESH)
    @pl.when(x < 2)
    def _():
        pl.semaphore_signal(barrier, inc=1, device_id=(relay_peer,), device_id_type=MESH)
    for k in steps:
        @pl.when(higher(k) & jnp.logical_not(hears_later(k)))
        def _(k=k):
            pl.semaphore_signal(barrier, inc=1, device_id=(columns[k],), device_id_type=MESH)

    get_gain = fetch(norm_gain, gain_ref, 1)
    group = z * 2 + y // 2
    member = x * 4 + (y % 2) * 2 + core
    get_row.wait()
    gather[group, pl.ds(member, 1)] = virtual_row[...].astype(F32)
    get_gain.wait()
    gain = gain_ref[...]
    get_features.wait()
    get_query = fetch(w_query, wq, 3)
    get_key = fetch(key_weight, wkv.at[:, pl.ds(0, WIDTH)], 4)
    get_value = fetch(value_weight, wkv.at[:, pl.ds(WIDTH, WIDTH)], 5)
    get_pairs = fetch(block_pairs, pairs, 6)
    get_partners = fetch(partner_blocks, partners, 7)
    get_masks = fetch(masks, mask_raw, 8)

    def partner(m, b):
        return partners[m, b]
    for block in range(BLOCKS):
        rows = pl.ds(block * BLK, BLK)
        normed[rows] = norm_rows(raw[rows].astype(F32), gain)

    def remote(src, dst, send, recv, peer):
        return pltpu.make_async_remote_copy(
            src_ref=src, dst_ref=dst, send_sem=send, recv_sem=recv, device_id=(peer,), device_id_type=MESH
        )

    def x_copy(r):
        c, part = r // PER_BLOCK, r % PER_BLOCK
        return remote(
            normed.at[pl.ds(r * RELAY, RELAY)],
            land.at[c, 1, pl.ds(part * RELAY, RELAY)],
            send_x.at[r], recv_x.at[r], x_peer,
        )

    def relay_copy(r):
        c, part = r // PER_BLOCK, r % PER_BLOCK
        return remote(
            land.at[c, 1, pl.ds(part * RELAY, RELAY)],
            land.at[c + 1, 2, pl.ds(part * RELAY, RELAY)],
            send_relay.at[r], recv_relay.at[r], relay_peer,
        )

    def y_copy(c):
        return remote(normed.at[pl.ds(c * BLK, BLK)], land.at[c, 0], send_y.at[c], recv_y.at[c], y_peer)

    copy_core = remote(normed, land_core, send_core.at[0], recv_core.at[0], core_peer)
    mine = gather.at[group, pl.ds(member, 1)]
    copy_plane = [remote(mine, mine, send_row.at[i], recv_row.at[i], peer) for i, peer in enumerate(plane)]
    eight = gather.at[group, pl.ds(pl.multiple_of(8 * (x // 2), 8), 8)]
    copy_across = remote(eight, eight, send_row.at[7], recv_row.at[7], relay_peer)
    sixteen = gather.at[group]

    def column_copy(k):
        return remote(sixteen, sixteen, send_row.at[7 + k], recv_row.at[7 + k], columns[k])

    def column_arrived(k):
        column_copy(16 - k).wait_recv()

    def tell_lower():
        @pl.when(x >= 2)
        def _():
            pl.semaphore_signal(entered.at[2], inc=1, device_id=(relay_peer,), device_id_type=MESH)
        @pl.when(rank == 11)
        def _():
            for k in (13, 14, 15):
                pl.semaphore_signal(token, inc=1, device_id=(columns[k],), device_id_type=MESH)
        for k in steps:
            @pl.when(jnp.logical_not(higher(k)) & jnp.logical_not(remote_eight & (rank + k == 16 + 7)))
            def _(k=k):
                crosses = jnp.where((rank >= 8) & (rank + k - 16 < 8), 1, 0)
                pl.semaphore_signal(entered.at[crosses], inc=1, device_id=(columns[k],), device_id_type=MESH)

    def tell_rank_seven():
        @pl.when(remote_eight)
        def _():
            pl.semaphore_wait(token, 1)
            seven = ranked(7)
            pl.semaphore_signal(entered.at[1], inc=1, device_id=(seven,), device_id_type=MESH)

    def send_lower():
        for k in steps:
            @pl.when(jnp.logical_not(higher(k)))
            def _(k=k):
                column_copy(k).start()

    def send_higher_near():
        @pl.when(rank % 8 < 7)
        def _():
            pl.semaphore_wait(entered.at[0], 7 - rank % 8)
        for k in range(1, 8):
            @pl.when(rank % 8 + k < 8)
            def _(k=k):
                column_copy(k).start()

    def send_higher_far():
        pl.semaphore_wait(entered.at[1], 8)
        for k in steps:
            @pl.when((rank + k >= 8) & higher(k))
            def _(k=k):
                column_copy(k).start()

    def send_bulk():
        x_copy(0).start()
        for copy in copy_plane:
            copy.start()
        for c in range(BLOCKS):
            for part in range(PER_BLOCK):
                if c or part:
                    x_copy(c * PER_BLOCK + part).start()
            y_copy(c).start()
        copy_core.start()

    def relay(half_block):
        for part in range(BLK // 2 // RELAY):
            r = half_block * (BLK // 2 // RELAY) + part
            x_copy(r).wait_recv()
            relay_copy(r).start()

    even, odd = lane_halves(BLK)
    ones = jnp.concatenate([even, odd], axis=0)

    def widen(v2):
        return jnp.concatenate([v2, ones], axis=1)

    def project(rows, place_k, place_v, blocks):
        for offset, place in ((0, place_k), (WIDTH, place_v)):
            for jj in range(0, PAIR, 2):
                part = dot(rows, wkv[:, offset + jj * BLK:offset + (jj + 2) * BLK])
                for j in range(jj, jj + 2):
                    for b in range(blocks):
                        piece = part[b * BLK:(b + 1) * BLK, (j - jj) * BLK:(j - jj + 1) * BLK].astype(BF)
                        ref = place(b, j)
                        ref[0:BLK] = piece * even
                        ref[BLK:2 * BLK] = piece * odd

    def own_queries():
        get_query.wait()
        for jj in range(0, PAIR, 2):
            part = dot(normed[...], wq[:, jj * BLK:(jj + 2) * BLK])
            for j in range(jj, jj + 2):
                for b in range(BLOCKS):
                    qs[j, b] = part[b * BLK:(b + 1) * BLK, (j - jj) * BLK:(j - jj + 1) * BLK].astype(BF)

    def own_keys_values():
        get_key.wait()
        get_value.wait()
        project(normed[...], lambda b, j: own_k.at[j, b], lambda b, j: own_v.at[j, b], BLOCKS)

    def spread_masks():
        get_masks.wait()
        get_pairs.wait()
        get_partners.wait()
        live = counts[0]
        for qb in range(BLOCKS):
            for kb in range(BLOCKS):
                slot = jnp.int32(0)
                for s in range(SLOTS):
                    slot = jnp.where((pairs[0, s] == qb) & (pairs[1, s] == kb), s, slot)
                alive = jnp.where(slot < live, 1, 0)
                keep[qb, kb] = (mask_raw[slot] * alive).astype(F32).astype(BF)

    def attend_local(pair_range):
        for j in pair_range:
            q = qs[j].reshape(ROWS, BLK)
            for kb in range(BLOCKS):
                s = scores(q, own_k[j, kb])
                for b in range(BLOCKS):
                    mask = keep[b, kb]
                    p = jnp.exp2(s[b * BLK:(b + 1) * BLK]).astype(BF)
                    weights[j, b * BLK:(b + 1) * BLK, kb * 2 * BLK:(kb + 1) * 2 * BLK] = p * jnp.concatenate(
                        [mask, mask], axis=1
                    )
        for j in pair_range:
            v = jnp.concatenate([widen(own_v[j, kb]) for kb in range(BLOCKS)], axis=0)
            near[j] = dot(weights[j], v).reshape(BLOCKS, BLK, 2 * BLK)

    def project_core():
        project(land_core[...], lambda b, j: core_k.at[b, j], lambda b, j: core_v.at[b, j], BLOCKS)

    def attend_core():
        block = [partner(0, b) for b in range(BLOCKS)]
        for j in range(PAIR):
            for b in range(BLOCKS):
                weights[j, b * BLK:(b + 1) * BLK, 0:2 * BLK] = jnp.exp2(
                    scores(qs[j, b], core_k[block[b], j])
                ).astype(BF)
        for j in range(PAIR):
            for b in range(BLOCKS):
                near[j, b] += dot(weights[j, b * BLK:(b + 1) * BLK, 0:2 * BLK], widen(core_v[block[b], j]))

    def far_step(c, sources):
        lo, hi = sources[0], sources[-1] + 1
        rows = land[c, lo:hi].reshape((hi - lo) * BLK, WIDTH)
        project(rows, lambda b, j: far_k.at[lo + b, j], lambda b, j: far_v.at[lo + b, j], hi - lo)
        for m in sources:
            block = c - 1 if m == 2 else c
            target = jnp.int32(0)
            for b in range(BLOCKS):
                target = jnp.where(partner(m + 1, b) == block, b, target)
            for j in range(PAIR):
                far_w[m, j] = jnp.exp2(scores(qs[j, target], far_k[m, j])).astype(BF)
        for m in sources:
            block = c - 1 if m == 2 else c
            for j in range(PAIR):
                far_acc[m, block, j] = dot(far_w[m, j], widen(far_v[m, j]))

    def arrive_relayed(c):
        for part in range(PER_BLOCK):
            relay_copy(c * PER_BLOCK + part).wait_recv()

    def virtual_nodes():
        even_v, odd_v = lane_halves(VIRTUAL)
        ones_v = jnp.concatenate([even_v, odd_v], axis=0)
        table = gather.reshape(256, BLK)
        state = jnp.concatenate([table[pl.ds(i, VIRTUAL, stride=4), :] for i in range(4)], axis=1)
        virtual_kv = dot(norm_rows(state, gain), wkv[...]).astype(BF)
        for j in range(PAIR):
            for offset, ref in ((0, virt_k), (WIDTH, virt_v)):
                piece = virtual_kv[:, offset + j * BLK:offset + (j + 1) * BLK]
                ref[j, 0:VIRTUAL] = piece * even_v
                ref[j, VIRTUAL:2 * VIRTUAL] = piece * odd_v
        for j in range(PAIR):
            s = scores(qs[j].reshape(ROWS, BLK), virt_k[j])
            weights[j, :, 0:BLK] = jnp.exp2(s).astype(BF)
        for j in range(PAIR):
            wide = jnp.concatenate([virt_v[j], ones_v], axis=1)
            near[j] += dot(weights[j, :, 0:BLK], wide).reshape(BLOCKS, BLK, 2 * BLK)

    def add_far():
        for j in range(PAIR):
            for b in range(BLOCKS):
                near[j, b] += far_acc[0, partner(1, b), j] + far_acc[1, partner(2, b), j]

    def finish():
        for b in range(BLOCKS):
            for j in range(PAIR):
                total = near[j, b] + far_acc[2, partner(3, b), j]
                out_ref[b * BLK:(b + 1) * BLK, j * BLK:(j + 1) * BLK] = (
                    total[:, 0:BLK] / total[:, BLK:2 * BLK]
                ).astype(BF)

    pl.semaphore_wait(barrier, 7 + x // 2 + rank - jnp.where(remote_eight, 1, 0))
    send_bulk()
    tell_lower()
    own_queries()
    own_keys_values()
    spread_masks()
    attend_local((0, 1))
    tell_rank_seven()
    for copy in copy_plane:
        copy.wait_recv()

    @pl.when(x < 2)
    def _():
        pl.semaphore_wait(entered.at[2], 1)
    copy_across.start()
    relay(0)
    attend_local((2, 3))
    relay(1)
    copy_core.wait_recv()
    project_core()
    copy_across.wait_recv()
    send_lower()
    relay(2)
    attend_core()
    y_copy(0).wait_recv()
    far_step(0, (0, 1))
    relay(3)
    send_higher_near()

    @pl.loop(1, BLOCKS)
    def _(c):
        @pl.when((z < 4) & (c == 2 - z // 2))
        def _():
            send_higher_far()

        y_copy(c).wait_recv()
        far_step(c, (0, 1))

        @pl.when(c < BLOCKS - 1)
        def _():
            relay(2 * c + 2)

        arrive_relayed(c - 1)
        far_step(c, (2,))

        @pl.when(c == 3)
        def _():
            for k in steps:
                column_arrived(k)
            virtual_nodes()

        @pl.when(c < BLOCKS - 1)
        def _():
            relay(2 * c + 3)

    for copy in copy_plane + [copy_across, copy_core]:
        copy.wait_send()
    for r in range(RELAYS):
        x_copy(r).wait_send()
    for c in range(BLOCKS):
        y_copy(c).wait_send()
    add_far()
    for r in range(RELAYS - PER_BLOCK):
        relay_copy(r).wait_send()
    for k in steps:
        column_copy(k).wait_send()
    arrive_relayed(BLOCKS - 1)
    far_step(BLOCKS, (2,))
    finish()
    for r in range(RELAYS - PER_BLOCK, RELAYS):
        relay_copy(r).wait_send()


def out_kernel(mixed, w_ref, out_ref, rows, sems):
    copies = []
    for b in range(BLOCKS):
        part = pl.ds(b * BLK, BLK)
        rows[part] = dot(mixed[part], w_ref[...]).astype(BF)
        copies.append(pltpu.make_async_copy(rows.at[part], out_ref.at[part], sems.at[b]))
        copies[b].start()
    for copy in copies:
        copy.wait()


def local(
    features, norm_gain, w_query, key_weight, value_weight, w_out, virtual_states, block_pairs, block_masks,
    pair_counts, partners,
):
    dma = pltpu.SemaphoreType.DMA
    hbm = pl.BlockSpec(memory_space=pltpu.HBM)
    mixed = pl.pallas_call(
        kernel,
        out_shape=jax.ShapeDtypeStruct((ROWS, WIDTH), BF),
        in_specs=[hbm] * 8 + [pl.BlockSpec(memory_space=pltpu.SMEM), hbm],
        out_specs=pl.BlockSpec(memory_space=pltpu.VMEM),
        scratch_shapes=[
            pltpu.VMEM((1, WIDTH), F32),
            pltpu.VMEM((1, BLK), BF),
            pltpu.SMEM((2, SLOTS), jnp.int32),
            pltpu.SMEM((4, BLOCKS), jnp.int32),
            pltpu.VMEM((ROWS, WIDTH), BF),
            pltpu.VMEM((ROWS, WIDTH), BF),
            pltpu.VMEM((WIDTH, WIDTH), BF),
            pltpu.VMEM((WIDTH, 2 * WIDTH), BF),
            pltpu.VMEM((SLOTS, BLK, BLK), jnp.int32),
            pltpu.VMEM((BLOCKS, BLOCKS, BLK, BLK), BF),
            pltpu.VMEM((PAIR, BLOCKS, BLK, BLK), BF),
            pltpu.VMEM((PAIR, BLOCKS, 2 * BLK, BLK), BF),
            pltpu.VMEM((PAIR, BLOCKS, 2 * BLK, BLK), BF),
            pltpu.VMEM((ROWS, WIDTH), BF),
            pltpu.VMEM((BLOCKS, PAIR, 2 * BLK, BLK), BF),
            pltpu.VMEM((BLOCKS, PAIR, 2 * BLK, BLK), BF),
            pltpu.VMEM((BLOCKS + 1, 3, BLK, WIDTH), BF),
            pltpu.VMEM((3, PAIR, 2 * BLK, BLK), BF),
            pltpu.VMEM((3, PAIR, 2 * BLK, BLK), BF),
            pltpu.VMEM((PAIR, BLK, BLK), BF),
            pltpu.VMEM((PAIR, BLK, BLK), BF),
            pltpu.VMEM((16, 16, BLK), F32),
            pltpu.VMEM((PAIR, BLOCKS, BLK, 2 * BLK), F32),
            pltpu.VMEM((3, BLOCKS, PAIR, BLK, 2 * BLK), F32),
            pltpu.VMEM((PAIR, ROWS, 8 * BLK), BF),
            pltpu.VMEM((3, PAIR, BLK, 2 * BLK), BF),
            dma((9,)),
            dma((23,)), dma((23,)),
            dma((1,)), dma((1,)),
            dma((BLOCKS,)), dma((BLOCKS,)),
            dma((RELAYS,)), dma((RELAYS,)),
            dma((RELAYS,)), dma((RELAYS,)),
            pltpu.SemaphoreType.REGULAR((3,)),
            pltpu.SemaphoreType.REGULAR,
        ],
        compiler_params=pltpu.CompilerParams(
            collective_id=0, has_side_effects=True, vmem_limit_bytes=54500 * 1024
        ),
        cost_estimate=pl.CostEstimate(flops=8_000_000_000, bytes_accessed=4_500_000, transcendentals=4_500_000),
        name="expander_layer",
    )(
        *(
            pltpu.with_memory_space_constraint(a, pltpu.HBM)
            for a in (
                features, norm_gain.reshape(1, WIDTH), w_query, key_weight, value_weight, virtual_states,
                block_pairs.T, block_masks,
            )
        ),
        pair_counts,
        pltpu.with_memory_space_constraint(partners.reshape(4, BLOCKS), pltpu.HBM),
    )
    vmem = pl.BlockSpec(memory_space=pltpu.VMEM)
    return pl.pallas_call(
        out_kernel,
        out_shape=jax.ShapeDtypeStruct((ROWS, WIDTH), BF),
        in_specs=[vmem, vmem],
        out_specs=hbm,
        scratch_shapes=[pltpu.VMEM((ROWS, WIDTH), BF), dma((BLOCKS,))],
        compiler_params=pltpu.CompilerParams(vmem_limit_bytes=8 * 1024 * 1024),
        cost_estimate=pl.CostEstimate(flops=270_000_000, bytes_accessed=1_600_000, transcendentals=0),
        name="out_projection",
    )(mixed, w_out)


def solution(mesh):
    placed = (
        P("nodes", None), P(), P(), P(), P(), P(), P("nodes", None), P("nodes", None), P("nodes", None, None),
        P("nodes"), P("nodes", None, None),
    )
    return jax.shard_map(local, mesh=mesh, in_specs=placed, out_specs=P("nodes", None), check_vma=False)
```
